32 devices in a mesh: section: 2 (over x), dp: 4 (over y, core), tensor: 4 (over z).
Axes of the slice: x: 2, y: 2, z: 4, core: 2. Of those that a mesh axis runs over, the one named last changes fastest.
Arguments:
- hidden: bfloat16 [2, 640, 8192], P('section', 'dp', 'tensor'), may hold values from -6 to 6
- w_query: bfloat16 [2, 8192, 4096], P('section', 'dp', 'tensor'), may hold values from -0.0625 to 0.0625
- key_weight_stack: bfloat16 [2, 8192, 1024], P('section', 'tensor', 'dp'), may hold values from -0.0625 to 0.0625
- value_weight_stack: bfloat16 [2, 8192, 1024], P('section', 'tensor', 'dp'), may hold values from -0.0625 to 0.0625
- image_tokens: bfloat16 [4, 128, 8192], P('dp', 'section', 'tensor'), may hold values from -6 to 6
- score_bias: float32 [640, 128], P('dp'), may hold values from -4 to 404, as said below
- gate_logit: float32 [2], P('section'), may hold values from 0.3 to 1.5
- cotangent: bfloat16 [2, 640, 4096], P('section', 'dp', 'tensor'), may hold values from -48 to 48
Outputs:
- gated_output: bfloat16 [2, 640, 4096], P('section', 'dp', 'tensor')
- image_grad: float32 [4, 128, 8192], P('dp', 'section', 'tensor')
The draws below stay inside these ranges and needn't reach their ends.
Inputs may be any that keep to these rules, and one draw needn't show every extreme that they name: `score_bias`: additive bias on the attention scores of each text token and image token.
All inputs are finite; a program needn't handle non-finite values.
Results may differ from the reference program's by a relative error of at most 0.0079.
Values may be sent and summed in bfloat16 or wider, within the bound.
A program may use at most 64 MiB of HBM per device.

```python
import jax
import jax.numpy as jnp
from jax import lax

MODEL_WIDTH = 8192
QUERY_HEADS = 32
KEY_VALUE_HEADS = 8
HEAD_SIZE = 128
BATCH_TOKENS = 160
IMAGE_TOKENS = 128
TOKENS = 640
IMAGES = 4
RELAY_SECTIONS = 2
N_DP = 4


def draw_score_bias(key, part):
    key = jax.random.fold_in(key, 11)
    values_base = jnp.clip(jax.random.normal(key, (TOKENS, IMAGE_TOKENS), jnp.float32), -4.0, 4.0)
    return values_base


def block_scale(stream_key, dims, shards, least, high):
    loudness, own = 1.0, jax.random.fold_in(stream_key, 6)
    for dim, blocks in shards:
        steps = jnp.exp(jax.random.uniform(jax.random.fold_in(own, dim), (blocks,), jnp.float32, least / len(shards), high / len(shards)))
        loudness = loudness * jnp.repeat(steps, dims[dim] // blocks).reshape([-1 if axis == dim else 1 for axis in range(len(dims))])
    return loudness


def normal_values(stream_key, dims, scale, most, shards=(), dtype=jnp.bfloat16):
    level = block_scale(stream_key, dims, shards, -0.22, 0.18) if shards else 1.0
    result = jax.random.normal(stream_key, dims, jnp.float32) * scale * level
    return jnp.minimum(jnp.maximum(result, -most), most).astype(dtype)


def setup_inputs(seed: int = 0) -> dict:
    key_list = jax.random.split(jax.random.key(seed), 9)
    return {
        "hidden": normal_values(key_list[0], (RELAY_SECTIONS, TOKENS, MODEL_WIDTH), 1.0, 6.0, ((0, 2), (1, 4), (2, 4))),
        "w_query": normal_values(key_list[1], (RELAY_SECTIONS, MODEL_WIDTH, QUERY_HEADS * HEAD_SIZE), MODEL_WIDTH ** -0.5, 0.0625, ((0, 2), (1, 4), (2, 4))),
        "key_weight_stack": normal_values(key_list[2], (RELAY_SECTIONS, MODEL_WIDTH, KEY_VALUE_HEADS * HEAD_SIZE), MODEL_WIDTH ** -0.5, 0.0625, ((0, 2), (1, 4), (2, 4))),
        "value_weight_stack": normal_values(key_list[3], (RELAY_SECTIONS, MODEL_WIDTH, KEY_VALUE_HEADS * HEAD_SIZE), MODEL_WIDTH ** -0.5, 0.0625, ((0, 2), (1, 4), (2, 4))),
        "image_tokens": normal_values(key_list[4], (IMAGES, IMAGE_TOKENS, MODEL_WIDTH), 1.0, 6.0, ((0, 4), (1, 2), (2, 4))),
        "score_bias": draw_score_bias(jax.random.fold_in(key_list[8], 71), 0),
        "gate_logit": jnp.clip(0.3 + 1.2 * jax.random.uniform(key_list[6], (RELAY_SECTIONS,), jnp.float32) ** block_scale(key_list[6], (RELAY_SECTIONS,), ((0, 2),), -0.2, 0.2), 0.3, 1.5),
        "cotangent": normal_values(key_list[7], (RELAY_SECTIONS, TOKENS, QUERY_HEADS * HEAD_SIZE), 8.0, 48.0, ((0, 2), (1, 4), (2, 4))),
    }


def rounded_values(values):
    return lax.optimization_barrier(values.astype(jnp.bfloat16)).astype(jnp.float32)


def reference(hidden, w_query, key_weight_stack, value_weight_stack, image_tokens, score_bias, gate_logit, cotangent):
    query_group_size = QUERY_HEADS // KEY_VALUE_HEADS
    scaling = HEAD_SIZE ** -0.5
    flat_images = image_tokens.reshape(N_DP * IMAGE_TOKENS, MODEL_WIDTH)
    bias_view = score_bias.reshape(N_DP, 1, 1, BATCH_TOKENS, IMAGE_TOKENS)

    def section_step(running, inputs):
        hidden_s, query_w, key_weight, value_weight, gate_s, cotangent_section = inputs
        query_input = jnp.dot(hidden_s, query_w, preferred_element_type=jnp.float32).astype(jnp.bfloat16)
        key_projected = jnp.dot(flat_images, key_weight, preferred_element_type=jnp.float32).astype(jnp.bfloat16)
        value_projected = jnp.dot(flat_images, value_weight, preferred_element_type=jnp.float32).astype(jnp.bfloat16)
        query_float = query_input.astype(jnp.float32).reshape(N_DP, BATCH_TOKENS, KEY_VALUE_HEADS, query_group_size, HEAD_SIZE)
        key_float = key_projected.astype(jnp.float32).reshape(N_DP, IMAGE_TOKENS, KEY_VALUE_HEADS, HEAD_SIZE)
        value_float = value_projected.astype(jnp.float32).reshape(N_DP, IMAGE_TOKENS, KEY_VALUE_HEADS, HEAD_SIZE)
        scores = jnp.einsum('ntkgh,nikh->nkgti', query_float, key_float) * scaling + bias_view
        row_max = jnp.max(scores, axis=-1, keepdims=True)
        exponent = jnp.exp(scores - row_max)
        attn_weights = exponent / jnp.sum(exponent, axis=-1, keepdims=True)
        weights_low = rounded_values(attn_weights)
        attended = jnp.einsum('nkgti,nikh->ntkgh', weights_low, value_float)
        scale_factor = jnp.tanh(gate_s)
        gated_out = (scale_factor * attended).astype(jnp.bfloat16).reshape(TOKENS, QUERY_HEADS * HEAD_SIZE)
        attended_gradient = rounded_values(scale_factor * cotangent_section.astype(jnp.float32)).reshape(N_DP, BATCH_TOKENS, KEY_VALUE_HEADS, query_group_size, HEAD_SIZE)
        value_gradient = jnp.einsum('nkgti,ntkgh->nikh', weights_low, attended_gradient).astype(jnp.bfloat16)
        grad_weights = jnp.einsum('ntkgh,nikh->nkgti', attended_gradient, value_float)
        grad_scores = attn_weights * (grad_weights - jnp.sum(attn_weights * grad_weights, axis=-1, keepdims=True))
        grad_low = rounded_values(grad_scores)
        key_gradient = (jnp.einsum('nkgti,ntkgh->nikh', grad_low, query_float) * scaling).astype(jnp.bfloat16)
        section_gradient = jnp.dot(key_gradient.reshape(N_DP * IMAGE_TOKENS, KEY_VALUE_HEADS * HEAD_SIZE), key_weight.T, preferred_element_type=jnp.float32)
        section_gradient = section_gradient + jnp.dot(value_gradient.reshape(N_DP * IMAGE_TOKENS, KEY_VALUE_HEADS * HEAD_SIZE), value_weight.T, preferred_element_type=jnp.float32)
        return running + section_gradient, gated_out

    initial = jnp.zeros((N_DP * IMAGE_TOKENS, MODEL_WIDTH), jnp.float32)
    summed, outputs = lax.scan(section_step, initial, (hidden, w_query, key_weight_stack, value_weight_stack, gate_logit, cotangent))
    return outputs, summed.reshape(N_DP, IMAGE_TOKENS, MODEL_WIDTH)
```

```python
import functools

import jax
import jax.numpy as jnp
from jax import lax
from jax.experimental import pallas as pl
from jax.experimental.pallas import tpu as pltpu
from jax.sharding import PartitionSpec as P

HEAD_SIZE = 128
QUERY_GROUP = 4
CORES = 2
BF16 = jnp.bfloat16
F32 = jnp.float32
NT = (((1,), (1,)), ((), ()))
TN = (((0,), (0,)), ((), ()))


def remote(src, dst, send_sem, recv_sem, device):
    return pltpu.make_async_remote_copy(
        src_ref=src,
        dst_ref=dst,
        send_sem=send_sem,
        recv_sem=recv_sem,
        device_id=device,
        device_id_type=pl.DeviceIdType.MESH,
    )


def kernel(
    sizes, hidden, w_query, key_w, value_w, image, bias, gate, cotangent, out, grad,
    wq, wkv, img, cot, hb, pb, kvr, kvs, qsib, qsr, qsend, qr, qacc, qs, gb, fsib, fsr, fsend, fr,
    load, ix_s, ix_r, iy_s, iy_r, ic_s, ic_r, hr_s, hl_s, h_r, hx_s, hx_r, p_s, p_r, kv_s, kv_r,
    qc_s, qc_r, qy_s, qy_r, g_s, g_r, gx_s, gx_r, fc_s, fc_r, f_s, f_r,
):
    S, D, T = sizes
    Y = D // CORES
    s, d, t = lax.axis_index("section"), lax.axis_index("dp"), lax.axis_index("tensor")
    y, c = d // CORES, d % CORES
    sibling = y * CORES + 1 - c
    rows = image.shape[0]
    image_count = S * rows
    kc = key_w.shape[1]
    width = wq.shape[1]
    feats = wq.shape[0]
    qtile = min(256, width)
    waits = []

    def load_copy(i, src, dst):
        copy = pltpu.make_async_copy(src, dst, load.at[i])
        copy.start()
        return copy

    own_rows = pl.ds(pl.multiple_of(d * image_count + s * rows, rows), rows)
    load_image = load_copy(0, image, img.at[own_rows])
    load_hidden = load_copy(1, hidden, hb.at[t])
    load_key = load_copy(2, key_w, wkv.at[:, pl.ds(0, kc)])
    load_value = load_copy(3, value_w, wkv.at[:, pl.ds(kc, kc)])
    load_query = load_copy(4, w_query, wq)
    load_cot = load_copy(5, cotangent, cot)

    others = [{"dp": lax.rem(d + j, D)} for j in range(1, D)]
    others += [{"tensor": lax.rem(t + j, T)} for j in range(1, T)]
    for i in range(1, S):
        for j in range(Y):
            others.append(
                {"section": lax.rem(s + i, S), "dp": lax.rem(y + j, Y) * CORES + c}
            )
    barrier = pltpu.get_barrier_semaphore()
    for device in others:
        pl.semaphore_signal(
            barrier, inc=1, device_id=device, device_id_type=pl.DeviceIdType.MESH
        )
    pl.semaphore_wait(barrier, len(others))

    load_image.wait()
    for i in range(1, S):
        to = lax.rem(s + i, S)
        copy = remote(
            img.at[own_rows], img.at[own_rows], ix_s.at[to], ix_r.at[s], {"section": to}
        )
        copy.start()
        waits.append(copy.wait_send)

    load_hidden.wait()

    def right(f):
        return remote(hb.at[f], hb.at[f], hr_s.at[f], h_r.at[f], {"tensor": t + 1})

    def left(f):
        return remote(hb.at[f], hb.at[f], hl_s.at[f], h_r.at[f], {"tensor": t - 1})

    def across(f):
        return remote(hb.at[f], hb.at[T + d], hx_s.at[f], hx_r.at[d], {"dp": f})

    def hidden_arrive(k):
        if k == 0:
            return
        pl.when(t - k >= 0)(lambda: right(t - k).wait_recv())
        pl.when(t + k < T)(lambda: left(t + k).wait_recv())

    def hidden_pass(k):
        if k < T - 1:
            pl.when((t - k >= 0) & (t + 1 < T))(lambda: right(t - k).start())
            pl.when((t + k < T) & (t >= 1))(lambda: left(t + k).start())
        if k == 0:
            pl.when(t != d)(lambda: across(t).start())
        else:
            pl.when((t - k >= 0) & (t - k != d))(lambda: across(t - k).start())
            pl.when((t + k < T) & (t + k != d))(lambda: across(t + k).start())

    hidden_pass(0)

    def image_block(n):
        return img.at[pl.ds(pl.multiple_of(n * image_count, image_count), image_count)]

    for i in range(1, S):
        src = lax.rem(s + i, S)
        block = img.at[pl.ds(pl.multiple_of(d * image_count + src * rows, rows), rows)]
        remote(block, block, ix_s.at[src], ix_r.at[src], {"section": src}).wait_recv()
    for j in range(1, Y):
        to = lax.rem(y + j, Y)
        copy = remote(
            image_block(d), image_block(d), iy_s.at[to], iy_r.at[y], {"dp": to * CORES + c}
        )
        copy.start()
        waits.append(copy.wait_send)

    def to_sibling(n, slot):
        copy = remote(image_block(n), image_block(n), ic_s.at[slot], ic_r.at[slot], {"dp": sibling})
        copy.start()
        waits.append(copy.wait_send)

    to_sibling(d, y)
    for j in range(1, Y):
        src = lax.rem(y + j, Y)
        n = src * CORES + c
        remote(
            image_block(n), image_block(n), iy_s.at[src], iy_r.at[src], {"dp": n}
        ).wait_recv()
        to_sibling(n, src)

    hidden_arrive(1)
    hidden_pass(1)

    for j in range(Y):
        n = j * CORES + 1 - c
        remote(
            image_block(n), image_block(n), ic_s.at[j], ic_r.at[j], {"dp": sibling}
        ).wait_recv()
    load_key.wait()
    load_value.wait()
    ptile = min(256, 2 * kc)

    @pl.loop(0, 2 * kc // ptile)
    def _(i):
        columns = pl.ds(pl.multiple_of(i * ptile, ptile), ptile)
        part = jnp.dot(img[...], wkv[:, columns], preferred_element_type=F32).astype(BF16)
        for n in range(D):
            pb[n, :, columns] = part[n * image_count : (n + 1) * image_count]

    for j in range(1, D):
        n = lax.rem(d + j, D)
        copy = remote(pb.at[n], pb.at[D + d], p_s.at[n], p_r.at[d], {"dp": n})
        copy.start()
        waits.append(copy.wait_send)

    for k in range(2, T - 1):
        hidden_arrive(k)
        hidden_pass(k)

    for j in range(1, D):
        n = lax.rem(d + j, D)
        remote(pb.at[n], pb.at[D + n], p_s.at[n], p_r.at[n], {"dp": n}).wait_recv()
    for j in range(1, T):
        f = lax.rem(t + j, T)
        copy = remote(
            pb.at[jnp.where(f == d, f, D + f)], kvr.at[t], kv_s.at[f], kv_r.at[t], {"tensor": f}
        )
        copy.start()
        waits.append(copy.wait_send)

    hidden_arrive(T - 1)
    hidden_pass(T - 1)

    load_query.wait()

    def tokens_of(n):
        if n is None:
            return hb.at[d]
        remote(hb.at[0], hb.at[T + n], hx_s.at[0], hx_r.at[n], {"dp": n}).wait_recv()
        return hb.at[T + n]

    order = list(range(1, Y)) + [0]
    for j in order:
        yy = lax.rem(y + j, Y)
        block = tokens_of(yy * CORES + 1 - c)

        @pl.loop(0, width // qtile)
        def _(i):
            columns = pl.ds(pl.multiple_of(i * qtile, qtile), qtile)
            qsib[yy, :, columns] = jnp.dot(
                block[...], wq[:, columns], preferred_element_type=F32
            ).astype(BF16)

        copy = remote(qsib.at[yy], qsr.at[yy], qc_s.at[yy], qc_r.at[yy], {"dp": sibling})
        copy.start()
        waits.append(copy.wait_send)
    for j in order:
        yy = lax.rem(y + j, Y)
        block = tokens_of(None if j == 0 else yy * CORES + c)
        remote(qsib.at[yy], qsr.at[yy], qc_s.at[yy], qc_r.at[yy], {"dp": sibling}).wait_recv()

        @pl.loop(0, width // qtile)
        def _(i):
            columns = pl.ds(pl.multiple_of(i * qtile, qtile), qtile)
            part = jnp.dot(block[...], wq[:, columns], preferred_element_type=F32)
            part = part + qsr[yy, :, columns].astype(F32)
            if j:
                qsend[yy, :, columns] = part.astype(BF16)
            else:
                qacc[:, columns] = part

        if j:
            copy = remote(
                qsend.at[yy], qr.at[y], qy_s.at[yy], qy_r.at[y], {"dp": yy * CORES + c}
            )
            copy.start()
            waits.append(copy.wait_send)

    total = pb[jnp.where(t == d, t, D + t)].astype(F32)
    for j in range(1, T):
        f = lax.rem(t + j, T)
        remote(kvr.at[f], kvr.at[f], kv_s.at[f], kv_r.at[f], {"tensor": f}).wait_recv()
        total = total + kvr[f].astype(F32)
    kvs[...] = total.astype(BF16)
    load_cot.wait()

    query = qacc[...]
    for j in range(1, Y):
        yy = lax.rem(y + j, Y)
        remote(
            qsend.at[yy], qr.at[yy], qy_s.at[yy], qy_r.at[yy], {"dp": yy * CORES + c}
        ).wait_recv()
        query = query + qr[yy].astype(F32)
    qs[...] = query.astype(BF16)

    scaling = HEAD_SIZE ** (-0.5)
    tokens = bias.shape[0]
    scale = jnp.tanh(jnp.full((1, HEAD_SIZE), gate[0], F32))
    bias_rows = jnp.concatenate([bias[...]] * QUERY_GROUP, axis=0)
    for k in range(kc // HEAD_SIZE):
        key = kvs[:, k * HEAD_SIZE : (k + 1) * HEAD_SIZE]
        value = kvs[:, kc + k * HEAD_SIZE : kc + (k + 1) * HEAD_SIZE]
        heads = [
            slice((k * QUERY_GROUP + g) * HEAD_SIZE, (k * QUERY_GROUP + g + 1) * HEAD_SIZE)
            for g in range(QUERY_GROUP)
        ]
        stacked = jnp.concatenate([qs[:, h] for h in heads], axis=0)
        above = jnp.concatenate([cot[:, h] for h in heads], axis=0)
        above = (scale * above.astype(F32)).astype(BF16)
        scores = lax.dot_general(stacked, key, NT, preferred_element_type=F32) * scaling
        scores = scores + bias_rows
        exponent = jnp.exp(scores - jnp.max(scores, axis=-1, keepdims=True))
        weights = exponent / jnp.sum(exponent, axis=-1, keepdims=True)
        low = weights.astype(BF16)
        attended = scale * jnp.dot(low, value, preferred_element_type=F32)
        for g, h in enumerate(heads):
            out[:, h] = attended[g * tokens : (g + 1) * tokens].astype(BF16)
        value_grad = lax.dot_general(low, above, TN, preferred_element_type=F32)
        grad_weights = lax.dot_general(above, value, NT, preferred_element_type=F32)
        mean = jnp.sum(weights * grad_weights, axis=-1, keepdims=True)
        grad_low = (weights * (grad_weights - mean)).astype(BF16)
        key_grad = lax.dot_general(grad_low, stacked, TN, preferred_element_type=F32) * scaling
        gb[t, :, k * HEAD_SIZE : (k + 1) * HEAD_SIZE] = key_grad.astype(BF16)
        gb[t, :, kc + k * HEAD_SIZE : kc + (k + 1) * HEAD_SIZE] = value_grad.astype(BF16)

    for j in range(1, T):
        f = lax.rem(t + j, T)
        copy = remote(gb.at[t], gb.at[t], g_s.at[f], g_r.at[t], {"tensor": f})
        copy.start()
        waits.append(copy.wait_send)

    def grad_across(f):
        return remote(gb.at[f], gb.at[T + d], gx_s.at[f], gx_r.at[d], {"dp": f})

    def grad_arrive(f):
        remote(gb.at[f], gb.at[f], g_s.at[f], g_r.at[f], {"tensor": f}).wait_recv()
        pl.when(f != d)(lambda: grad_across(f).start())

    pl.when(t != d)(lambda: grad_across(t).start())
    for k in range(1, T):
        pl.when(t - k >= 0)(functools.partial(grad_arrive, t - k))
        pl.when(t + k < T)(functools.partial(grad_arrive, t + k))

    def grads_of(n):
        if n is None:
            return gb[d]
        remote(gb.at[0], gb.at[T + n], gx_s.at[0], gx_r.at[n], {"dp": n}).wait_recv()
        return gb[T + n]

    ftile = min(512, feats)
    for j in order:
        yy = lax.rem(y + j, Y)
        block = grads_of(yy * CORES + 1 - c)

        @pl.loop(0, feats // ftile)
        def _(i):
            columns = pl.ds(pl.multiple_of(i * ftile, ftile), ftile)
            fsib[yy, :, columns] = lax.dot_general(
                block, wkv[columns, :], NT, preferred_element_type=F32
            ).astype(BF16)

        copy = remote(fsib.at[yy], fsr.at[yy], fc_s.at[yy], fc_r.at[yy], {"dp": sibling})
        copy.start()
        waits.append(copy.wait_send)
    sections = list(range(1, S)) + [0]
    for j in order:
        yy = lax.rem(y + j, Y)
        block = grads_of(None if j == 0 else yy * CORES + c)
        remote(fsib.at[yy], fsr.at[yy], fc_s.at[yy], fc_r.at[yy], {"dp": sibling}).wait_recv()

        @pl.loop(0, feats // ftile)
        def _(i):
            columns = pl.ds(pl.multiple_of(i * ftile, ftile), ftile)
            part = lax.dot_general(block, wkv[columns, :], NT, preferred_element_type=F32)
            part = part + fsr[yy, :, columns].astype(F32)
            fsend[yy, :, columns] = part

        for i in sections:
            if i == 0 and j == 0:
                continue
            ss = lax.rem(s + i, S)
            span = pl.ds(pl.multiple_of(ss * rows, rows), rows)
            fsib_out = fr.at[0, yy, ss]
            fsib_out[...] = fsend[yy, span, :].astype(BF16)
            copy = remote(
                fsib_out, fr.at[1, y, s], f_s.at[yy, ss], f_r.at[y, s],
                {"section": ss, "dp": yy * CORES + c},
            )
            copy.start()
            waits.append(copy.wait_send)
    result = fsend[y, pl.ds(pl.multiple_of(s * rows, rows), rows), :]
    for j in order:
        yy = lax.rem(y + j, Y)
        for i in sections:
            if i == 0 and j == 0:
                continue
            ss = lax.rem(s + i, S)
            slot = fr.at[1, yy, ss]
            remote(
                slot, slot, f_s.at[yy, ss], f_r.at[yy, ss],
                {"section": ss, "dp": yy * CORES + c},
            ).wait_recv()
            result = result + slot[...].astype(F32)
    grad[...] = result

    for wait in waits:
        wait()
    for k in range(T):
        if k < T - 1:
            pl.when((t - k >= 0) & (t + 1 < T))(lambda: right(t - k).wait_send())
            pl.when((t + k < T) & (t >= 1))(lambda: left(t + k).wait_send())
    for f in range(T):
        pl.when(f != d)(lambda: across(f).wait_send())
        pl.when(f != d)(lambda: grad_across(f).wait_send())


def local(sizes, hidden, w_query, key_w, value_w, image, bias, gate, cotangent):
    S, D, T = sizes
    Y = D // CORES
    tokens, feats = hidden.shape[1:]
    width = w_query.shape[2]
    kc = key_w.shape[2]
    rows = image.shape[1]
    images = S * rows
    sem = lambda *n: pltpu.SemaphoreType.DMA(n)
    any_space = pl.BlockSpec(memory_space=pl.ANY)
    vmem = pl.BlockSpec(memory_space=pltpu.VMEM)
    smem = pl.BlockSpec(memory_space=pltpu.SMEM)
    out, grad = pl.pallas_call(
        functools.partial(kernel, sizes),
        out_shape=(
            jax.ShapeDtypeStruct((tokens, width), BF16),
            jax.ShapeDtypeStruct((rows, feats), F32),
        ),
        in_specs=[any_space] * 5 + [vmem, smem, any_space],
        out_specs=(vmem, vmem),
        scratch_shapes=[
            pltpu.VMEM((feats, width), BF16),
            pltpu.VMEM((feats, 2 * kc), BF16),
            pltpu.VMEM((D * images, feats), BF16),
            pltpu.VMEM((tokens, width), BF16),
            pltpu.VMEM((T + D, tokens, feats), BF16),
            pltpu.VMEM((2 * D, images, 2 * kc), BF16),
            pltpu.VMEM((T, images, 2 * kc), BF16),
            pltpu.VMEM((images, 2 * kc), BF16),
            pltpu.VMEM((Y, tokens, width), BF16),
            pltpu.VMEM((Y, tokens, width), BF16),
            pltpu.VMEM((Y, tokens, width), BF16),
            pltpu.VMEM((Y, tokens, width), BF16),
            pltpu.VMEM((tokens, width), F32),
            pltpu.VMEM((tokens, width), BF16),
            pltpu.VMEM((T + D, images, 2 * kc), BF16),
            pltpu.VMEM((Y, images, feats), BF16),
            pltpu.VMEM((Y, images, feats), BF16),
            pltpu.VMEM((Y, images, feats), F32),
            pltpu.VMEM((2, Y, S, rows, feats), BF16),
            sem(6),
            sem(S), sem(S), sem(Y), sem(Y), sem(Y), sem(Y),
            sem(T), sem(T), sem(T), sem(T), sem(D),
            sem(D), sem(D), sem(T), sem(T),
            sem(Y), sem(Y), sem(Y), sem(Y),
            sem(T), sem(T), sem(T), sem(D),
            sem(Y), sem(Y), sem(Y, S), sem(Y, S),
        ],
        compiler_params=pltpu.CompilerParams(
            collective_id=0, has_side_effects=True, vmem_limit_bytes=52 * 1024 * 1024
        ),
    )(hidden[0], w_query[0], key_w[0], value_w[0], image[0], bias, gate, cotangent[0])
    return out[None], grad[None]


def solution(mesh):
    sizes = tuple(mesh.shape[name] for name in ("section", "dp", "tensor"))
    assert sizes[1] == sizes[2] and sizes[1] % CORES == 0
    in_specs = (
        P("section", "dp", "tensor"),
        P("section", "dp", "tensor"),
        P("section", "tensor", "dp"),
        P("section", "tensor", "dp"),
        P("dp", "section", "tensor"),
        P("dp", None),
        P("section"),
        P("section", "dp", "tensor"),
    )
    out_specs = (P("section", "dp", "tensor"), P("dp", "section", "tensor"))
    return jax.shard_map(
        functools.partial(local, sizes),
        mesh=mesh, in_specs=in_specs, out_specs=out_specs, check_vma=False,
    )
```

```python
import functools

import jax
import jax.numpy as jnp
from jax import lax
from jax.experimental import pallas as pl
from jax.experimental.pallas import tpu as pltpu
from jax.sharding import PartitionSpec as P

HEAD_SIZE = 128
QUERY_GROUP = 4
HIDDEN_PARTS = 2
GRAD_PARTS = 2
CORES = 2
BF16 = jnp.bfloat16
F32 = jnp.float32
NT = (((1,), (1,)), ((), ()))
TN = (((0,), (0,)), ((), ()))


def remote(src, dst, send_sem, recv_sem, device):
    return pltpu.make_async_remote_copy(
        src_ref=src,
        dst_ref=dst,
        send_sem=send_sem,
        recv_sem=recv_sem,
        device_id=device,
        device_id_type=pl.DeviceIdType.MESH,
    )


def kernel(
    sizes, hidden, w_query, key_w, value_w, image, bias, gate, cotangent, out, grad,
    wq, wkv, img, cot, hb, pb, kvr, kvs, qsib, qsr, qsend, qr, qacc, above, wgrad, lows, gb, fsib, fsr, fsum, fsend, fr,
    load, ix_s, ix_r, iy_s, iy_r, ic_s, ic_r, hr_s, hl_s, h_r, hx_s, hx_r, p_s, p_r, kv_s, kv_r,
    qc_s, qc_r, qy_s, qy_r, g_s, g_r, gx_s, gx_r, fc_s, fc_r, f_s, f_r,
):
    S, D, T = sizes
    Y = D // CORES
    s, d, t = lax.axis_index("section"), lax.axis_index("dp"), lax.axis_index("tensor")
    y, c = d // CORES, d % CORES
    sibling = y * CORES + 1 - c
    rows = image.shape[0]
    image_count = S * rows
    kc = key_w.shape[1]
    width = wq.shape[1]
    feats = wq.shape[0]
    heads_here = kc // HEAD_SIZE
    pair = 2 * HEAD_SIZE
    span = QUERY_GROUP * HEAD_SIZE
    tokens = bias.shape[0]
    part_rows = tokens // HIDDEN_PARTS
    part_feats = feats // GRAD_PARTS
    waits = []

    def load_copy(i, src, dst):
        copy = pltpu.make_async_copy(src, dst, load.at[i])
        copy.start()
        return copy

    own_rows = pl.ds(pl.multiple_of(d * image_count + s * rows, rows), rows)
    load_image = load_copy(0, image, img.at[own_rows])
    load_hidden = load_copy(1, hidden, hb.at[t])
    load_query = load_copy(2, w_query, wq)
    load_cot = load_copy(3, cotangent, cot)
    load_pairs = []
    for k in range(heads_here):
        head = pl.ds(k * HEAD_SIZE, HEAD_SIZE)
        load_pairs += [
            load_copy(4 + 2 * k, key_w.at[:, head], wkv.at[:, pl.ds(k * pair, HEAD_SIZE)]),
            load_copy(
                5 + 2 * k, value_w.at[:, head], wkv.at[:, pl.ds(k * pair + HEAD_SIZE, HEAD_SIZE)]
            ),
        ]

    others = [{"dp": lax.rem(d + j, D)} for j in range(1, D)]
    others += [{"tensor": lax.rem(t + j, T)} for j in range(1, T)]
    for i in range(1, S):
        for j in range(Y):
            others.append(
                {"section": lax.rem(s + i, S), "dp": lax.rem(y + j, Y) * CORES + c}
            )
    barrier = pltpu.get_barrier_semaphore()
    for device in others:
        pl.semaphore_signal(
            barrier, inc=1, device_id=device, device_id_type=pl.DeviceIdType.MESH
        )
    pl.semaphore_wait(barrier, len(others))

    load_image.wait()
    for i in range(1, S):
        to = lax.rem(s + i, S)
        copy = remote(
            img.at[own_rows], img.at[own_rows], ix_s.at[to], ix_r.at[s], {"section": to}
        )
        copy.start()
        waits.append(copy.wait_send)

    load_hidden.wait()

    def piece(f, h):
        return hb.at[f, pl.ds(h * part_rows, part_rows)]

    def right(f, h):
        return remote(piece(f, h), piece(f, h), hr_s.at[f, h], h_r.at[f, h], {"tensor": t + 1})

    def left(f, h):
        return remote(piece(f, h), piece(f, h), hl_s.at[f, h], h_r.at[f, h], {"tensor": t - 1})

    def across(f, h):
        return remote(piece(f, h), piece(T + d, h), hx_s.at[f, h], hx_r.at[d, h], {"dp": f})

    def hidden_arrive(k, h):
        pl.when(t - k >= 0)(lambda: right(t - k, h).wait_recv())
        pl.when(t + k < T)(lambda: left(t + k, h).wait_recv())

    def hidden_pass(k, h):
        if k < T - 1:
            pl.when((t - k >= 0) & (t + 1 < T))(lambda: right(t - k, h).start())
            pl.when((t + k < T) & (t >= 1))(lambda: left(t + k, h).start())
        if k:
            pl.when((t - k >= 0) & (t - k != d))(lambda: across(t - k, h).start())
            pl.when((t + k < T) & (t + k != d))(lambda: across(t + k, h).start())

    def hidden_step(k, h):
        hidden_arrive(k, h)
        hidden_pass(k, h)

    for h in range(HIDDEN_PARTS):
        hidden_pass(0, h)

    def image_block(n):
        return img.at[pl.ds(pl.multiple_of(n * image_count, image_count), image_count)]

    for i in range(1, S):
        src = lax.rem(s + i, S)
        block = img.at[pl.ds(pl.multiple_of(d * image_count + src * rows, rows), rows)]
        remote(block, block, ix_s.at[src], ix_r.at[src], {"section": src}).wait_recv()
    for j in range(1, Y):
        to = lax.rem(y + j, Y)
        copy = remote(
            image_block(d), image_block(d), iy_s.at[to], iy_r.at[y], {"dp": to * CORES + c}
        )
        copy.start()
        waits.append(copy.wait_send)

    def to_sibling(n, slot):
        copy = remote(image_block(n), image_block(n), ic_s.at[slot], ic_r.at[slot], {"dp": sibling})
        copy.start()
        waits.append(copy.wait_send)

    to_sibling(d, y)
    for h in range(HIDDEN_PARTS):
        pl.when(t != d)(lambda: across(t, h).start())
    for h in range(HIDDEN_PARTS):
        hidden_step(1, h)
    for j in range(1, Y):
        src = lax.rem(y + j, Y)
        n = src * CORES + c
        remote(
            image_block(n), image_block(n), iy_s.at[src], iy_r.at[src], {"dp": n}
        ).wait_recv()
        to_sibling(n, src)

    for k in range(2, T - 1):
        hidden_step(k, 0)
    for j in range(Y):
        n = j * CORES + 1 - c
        remote(
            image_block(n), image_block(n), ic_s.at[j], ic_r.at[j], {"dp": sibling}
        ).wait_recv()
    for load_pair in load_pairs:
        load_pair.wait()
    ptile = min(256, 2 * kc)

    @pl.loop(0, 2 * kc // ptile)
    def _(i):
        columns = pl.ds(pl.multiple_of(i * ptile, ptile), ptile)
        part = jnp.dot(img[...], wkv[:, columns], preferred_element_type=F32).astype(BF16)
        for n in range(D):
            pb[n, :, columns] = part[n * image_count : (n + 1) * image_count]

    for j in range(1, D):
        n = lax.rem(d + j, D)
        copy = remote(pb.at[n], pb.at[D + d], p_s.at[n], p_r.at[d], {"dp": n})
        copy.start()
        waits.append(copy.wait_send)

    for k in range(2, T - 1):
        for h in range(1, HIDDEN_PARTS):
            hidden_step(k, h)
    for h in range(HIDDEN_PARTS):
        hidden_step(T - 1, h)

    load_query.wait()

    def tokens_of(n):
        if n is None:
            return hb.at[d]
        for h in range(HIDDEN_PARTS):
            remote(
                piece(0, h), piece(T + n, h), hx_s.at[0, h], hx_r.at[n, h], {"dp": n}
            ).wait_recv()
        return hb.at[T + n]

    def project(block, k):
        columns = slice(k * span, (k + 1) * span)
        return jnp.dot(block[...], wq[:, columns], preferred_element_type=F32)

    def query_to_sibling(yy, k):
        return remote(
            qsib.at[yy, k], qsr.at[yy, k], qc_s.at[yy, k], qc_r.at[yy, k], {"dp": sibling}
        )

    def query_to_chip(yy, k, slot):
        return remote(
            qsend.at[yy, k], qr.at[slot, k], qy_s.at[yy, k], qy_r.at[slot, k],
            {"dp": yy * CORES + c},
        )

    order = [0] + list(range(1, Y))
    for j in order:
        yy = lax.rem(y + j, Y)
        block = tokens_of(yy * CORES + 1 - c)
        for k in range(heads_here):
            qsib[yy, k] = project(block, k).astype(BF16)
            query_to_sibling(yy, k).start()
            waits.append(query_to_sibling(yy, k).wait_send)
        if j == 0:
            block = hb.at[d]
            for k in range(heads_here):
                qacc[k] = project(block, k)
            continue
        block = tokens_of(yy * CORES + c)
        for k in range(heads_here):
            part = project(block, k)
            query_to_sibling(yy, k).wait_recv()
            qsend[yy, k] = (part + qsr[yy, k].astype(F32)).astype(BF16)
            query_to_chip(yy, k, y).start()
            waits.append(query_to_chip(yy, k, y).wait_send)

    for j in range(1, D):
        n = lax.rem(d + j, D)
        remote(pb.at[n], pb.at[D + n], p_s.at[n], p_r.at[n], {"dp": n}).wait_recv()
    for j in range(1, T):
        f = lax.rem(t + j, T)
        copy = remote(
            pb.at[jnp.where(f == d, f, D + f)], kvr.at[t], kv_s.at[f], kv_r.at[t], {"tensor": f}
        )
        copy.start()
        waits.append(copy.wait_send)

    load_cot.wait()
    scale = jnp.tanh(jnp.full((1, HEAD_SIZE), gate[0], F32))
    bias_rows = jnp.concatenate([bias[...]] * QUERY_GROUP, axis=0)

    def stack(ref, k):
        first = k * span
        return jnp.concatenate(
            [
                ref[:, first + g * HEAD_SIZE : first + (g + 1) * HEAD_SIZE]
                for g in range(QUERY_GROUP)
            ],
            axis=0,
        )

    for k in range(heads_here):
        above[k] = (scale * stack(cot, k).astype(F32)).astype(BF16)
        query_to_sibling(y, k).wait_recv()
        qacc[k] = qacc[k] + qsr[y, k].astype(F32)
    total = pb[jnp.where(t == d, t, D + t)].astype(F32)
    for j in range(1, T):
        f = lax.rem(t + j, T)
        remote(kvr.at[f], kvr.at[f], kv_s.at[f], kv_r.at[f], {"tensor": f}).wait_recv()
        total = total + kvr[f].astype(F32)
    kvs[...] = total.astype(BF16)
    for k in range(heads_here):
        value = kvs[:, k * pair + HEAD_SIZE : (k + 1) * pair]
        wgrad[k] = lax.dot_general(above[k], value, NT, preferred_element_type=F32)

    scaling = HEAD_SIZE ** (-0.5)

    def grad_piece(f, k):
        return gb.at[f, :, pl.ds(k * pair, pair)]

    def grad_along(f, k, slot, to):
        return remote(
            grad_piece(slot, k), grad_piece(slot, k), g_s.at[f, k], g_r.at[slot, k], {"tensor": to}
        )

    def grad_across(f, k):
        return remote(
            grad_piece(f, k), grad_piece(T + d, k), gx_s.at[f, k], gx_r.at[d, k], {"dp": f}
        )

    for k in range(heads_here):
        key = kvs[:, k * pair : k * pair + HEAD_SIZE]
        query = qacc[k]
        for j in range(1, Y):
            yy = lax.rem(y + j, Y)
            query_to_chip(yy, k, yy).wait_recv()
            query = query + qr[yy, k].astype(F32)
        query = query.astype(BF16)
        stacked = jnp.concatenate(
            [query[:, g * HEAD_SIZE : (g + 1) * HEAD_SIZE] for g in range(QUERY_GROUP)], axis=0
        )
        scores = lax.dot_general(stacked, key, NT, preferred_element_type=F32) * scaling
        scores = scores + bias_rows
        exponent = jnp.exp(scores - jnp.max(scores, axis=-1, keepdims=True))
        weights = exponent / jnp.sum(exponent, axis=-1, keepdims=True)
        low = weights.astype(BF16)
        lows[k] = low
        value_grad = lax.dot_general(low, above[k], TN, preferred_element_type=F32)
        grad_weights = wgrad[k]
        mean = jnp.sum(weights * grad_weights, axis=-1, keepdims=True)
        grad_low = (weights * (grad_weights - mean)).astype(BF16)
        key_grad = lax.dot_general(grad_low, stacked, TN, preferred_element_type=F32) * scaling
        gb[t, :, k * pair : k * pair + HEAD_SIZE] = key_grad.astype(BF16)
        gb[t, :, k * pair + HEAD_SIZE : (k + 1) * pair] = value_grad.astype(BF16)
        for j in range(1, T):
            f = lax.rem(t + j, T)
            grad_along(f, k, t, f).start()
            waits.append(grad_along(f, k, t, f).wait_send)
        pl.when(t != d)(lambda: grad_across(t, k).start())

    for k in range(heads_here):
        value = kvs[:, k * pair + HEAD_SIZE : (k + 1) * pair]
        attended = scale * jnp.dot(lows[k], value, preferred_element_type=F32)
        for g in range(QUERY_GROUP):
            first = k * span + g * HEAD_SIZE
            out[:, first : first + HEAD_SIZE] = attended[g * tokens : (g + 1) * tokens].astype(BF16)

    def grad_arrive(f, k):
        grad_along(f, k, f, f).wait_recv()
        pl.when(f != d)(lambda: grad_across(f, k).start())

    for k in range(heads_here):
        for i in range(1, T):
            pl.when(t - i >= 0)(functools.partial(grad_arrive, t - i, k))
            pl.when(t + i < T)(functools.partial(grad_arrive, t + i, k))

    def grads_of(n):
        if n is None:
            return gb[d]
        for k in range(heads_here):
            remote(
                grad_piece(0, k), grad_piece(T + n, k), gx_s.at[0, k], gx_r.at[n, k], {"dp": n}
            ).wait_recv()
        return gb[T + n]

    def back(block, h):
        weights_part = wkv[h * part_feats : (h + 1) * part_feats, :]
        return lax.dot_general(block, weights_part, NT, preferred_element_type=F32)

    def image_to_sibling(yy, h):
        return remote(
            fsib.at[yy, h], fsr.at[yy, h], fc_s.at[yy, h], fc_r.at[yy, h], {"dp": sibling}
        )

    def image_to_owner(yy, ss, h, slot_y, slot_s):
        return remote(
            fsend.at[yy, ss, h], fr.at[slot_y, slot_s, h],
            f_s.at[yy, ss, h], f_r.at[slot_y, slot_s, h],
            {"section": ss, "dp": yy * CORES + c},
        )

    order = list(range(1, Y)) + [0]
    sections = list(range(1, S)) + [0]
    for j in order:
        yy = lax.rem(y + j, Y)
        block = grads_of(yy * CORES + 1 - c)
        for h in range(GRAD_PARTS):
            fsib[yy, h] = back(block, h).astype(BF16)
            image_to_sibling(yy, h).start()
            waits.append(image_to_sibling(yy, h).wait_send)
    for j in order:
        yy = lax.rem(y + j, Y)
        block = grads_of(None if j == 0 else yy * CORES + c)
        for h in range(GRAD_PARTS):
            part = back(block, h)
            image_to_sibling(yy, h).wait_recv()
            fsum[...] = part + fsr[yy, h].astype(F32)
            for i in sections:
                ss = lax.rem(s + i, S)
                mine = fsum[pl.ds(pl.multiple_of(ss * rows, rows), rows), :]
                if i == 0 and j == 0:
                    grad[:, h * part_feats : (h + 1) * part_feats] = mine
                    continue
                fsend[yy, ss, h] = mine.astype(BF16)
                image_to_owner(yy, ss, h, y, s).start()
                waits.append(image_to_owner(yy, ss, h, y, s).wait_send)
    for h in range(GRAD_PARTS):
        columns = slice(h * part_feats, (h + 1) * part_feats)
        result = grad[:, columns]
        for j in order:
            yy = lax.rem(y + j, Y)
            for i in sections:
                if i == 0 and j == 0:
                    continue
                ss = lax.rem(s + i, S)
                image_to_owner(yy, ss, h, yy, ss).wait_recv()
                result = result + fr[yy, ss, h].astype(F32)
        grad[:, columns] = result

    for wait in waits:
        wait()
    for h in range(HIDDEN_PARTS):
        for k in range(T - 1):
            pl.when((t - k >= 0) & (t + 1 < T))(lambda: right(t - k, h).wait_send())
            pl.when((t + k < T) & (t >= 1))(lambda: left(t + k, h).wait_send())
        for f in range(T):
            pl.when(f != d)(lambda: across(f, h).wait_send())
    for k in range(heads_here):
        for f in range(T):
            pl.when(f != d)(lambda: grad_across(f, k).wait_send())


def local(sizes, hidden, w_query, key_w, value_w, image, bias, gate, cotangent):
    S, D, T = sizes
    Y = D // CORES
    tokens, feats = hidden.shape[1:]
    width = w_query.shape[2]
    kc = key_w.shape[2]
    rows = image.shape[1]
    images = S * rows
    heads = kc // HEAD_SIZE
    span = QUERY_GROUP * HEAD_SIZE
    part_feats = feats // GRAD_PARTS
    sem = lambda *n: pltpu.SemaphoreType.DMA(n)
    any_space = pl.BlockSpec(memory_space=pl.ANY)
    vmem = pl.BlockSpec(memory_space=pltpu.VMEM)
    smem = pl.BlockSpec(memory_space=pltpu.SMEM)
    out, grad = pl.pallas_call(
        functools.partial(kernel, sizes),
        out_shape=(
            jax.ShapeDtypeStruct((tokens, width), BF16),
            jax.ShapeDtypeStruct((rows, feats), F32),
        ),
        in_specs=[any_space] * 5 + [vmem, smem, any_space],
        out_specs=(vmem, vmem),
        scratch_shapes=[
            pltpu.VMEM((feats, width), BF16),
            pltpu.VMEM((feats, 2 * kc), BF16),
            pltpu.VMEM((D * images, feats), BF16),
            pltpu.VMEM((tokens, width), BF16),
            pltpu.VMEM((T + D, tokens, feats), BF16),
            pltpu.VMEM((2 * D, images, 2 * kc), BF16),
            pltpu.VMEM((T, images, 2 * kc), BF16),
            pltpu.VMEM((images, 2 * kc), BF16),
            pltpu.VMEM((Y, heads, tokens, span), BF16),
            pltpu.VMEM((Y, heads, tokens, span), BF16),
            pltpu.VMEM((Y, heads, tokens, span), BF16),
            pltpu.VMEM((Y, heads, tokens, span), BF16),
            pltpu.VMEM((heads, tokens, span), F32),
            pltpu.VMEM((heads, QUERY_GROUP * tokens, HEAD_SIZE), BF16),
            pltpu.VMEM((heads, QUERY_GROUP * tokens, images), F32),
            pltpu.VMEM((heads, QUERY_GROUP * tokens, images), BF16),
            pltpu.VMEM((T + D, images, 2 * kc), BF16),
            pltpu.VMEM((Y, GRAD_PARTS, images, part_feats), BF16),
            pltpu.VMEM((Y, GRAD_PARTS, images, part_feats), BF16),
            pltpu.VMEM((images, part_feats), F32),
            pltpu.VMEM((Y, S, GRAD_PARTS, rows, part_feats), BF16),
            pltpu.VMEM((Y, S, GRAD_PARTS, rows, part_feats), BF16),
            sem(4 + 2 * heads),
            sem(S), sem(S), sem(Y), sem(Y), sem(Y), sem(Y),
            sem(T, HIDDEN_PARTS), sem(T, HIDDEN_PARTS), sem(T, HIDDEN_PARTS),
            sem(T, HIDDEN_PARTS), sem(D, HIDDEN_PARTS),
            sem(D), sem(D), sem(T), sem(T),
            sem(Y, heads), sem(Y, heads), sem(Y, heads), sem(Y, heads),
            sem(T, heads), sem(T, heads), sem(T, heads), sem(D, heads),
            sem(Y, GRAD_PARTS), sem(Y, GRAD_PARTS),
            sem(Y, S, GRAD_PARTS), sem(Y, S, GRAD_PARTS),
        ],
        compiler_params=pltpu.CompilerParams(
            collective_id=0, has_side_effects=True, vmem_limit_bytes=64 * 1024 * 1024 - 64 * 1024
        ),
    )(hidden[0], w_query[0], key_w[0], value_w[0], image[0], bias, gate, cotangent[0])
    return out[None], grad[None]


def solution(mesh):
    sizes = tuple(mesh.shape[name] for name in ("section", "dp", "tensor"))
    assert sizes[1] == sizes[2] and sizes[1] % CORES == 0
    in_specs = (
        P("section", "dp", "tensor"),
        P("section", "dp", "tensor"),
        P("section", "tensor", "dp"),
        P("section", "tensor", "dp"),
        P("dp", "section", "tensor"),
        P("dp", None),
        P("section"),
        P("section", "dp", "tensor"),
    )
    out_specs = (P("section", "dp", "tensor"), P("dp", "section", "tensor"))
    return jax.shard_map(
        functools.partial(local, sizes),
        mesh=mesh, in_specs=in_specs, out_specs=out_specs, check_vma=False,
    )
```

```python
import functools

import jax
import jax.numpy as jnp
from jax import lax
from jax.experimental import pallas as pl
from jax.experimental.pallas import tpu as pltpu
from jax.sharding import PartitionSpec as P

HEAD_SIZE = 128
QUERY_GROUP = 4
VMEM_BYTES = 64 * 1024 * 1024 - 64 * 1024
HALVES = 2
COLUMN_PARTS = 2
PIECES = HALVES * COLUMN_PARTS
GRAD_PARTS = 2
CORES = 2
BF16 = jnp.bfloat16
F32 = jnp.float32
NT = (((1,), (1,)), ((), ()))
TN = (((0,), (0,)), ((), ()))


def remote(src, dst, send_sem, recv_sem, device):
    return pltpu.make_async_remote_copy(
        src_ref=src,
        dst_ref=dst,
        send_sem=send_sem,
        recv_sem=recv_sem,
        device_id=device,
        device_id_type=pl.DeviceIdType.MESH,
    )


def kernel(
    sizes, hidden, w_query, key_w, value_w, image, bias_in, gate, cotangent, out, grad,
    bias, wq, wkv, img, cot, hb, pb, kvr, kvs, qsib, qsr, qsend, qr, qfull, qacc, lows, gacc, gb, fsib, fsr, ffull, fsum, fsend, fr,
    load, ix_s, ix_r, iy_s, iy_r, ic_s, ic_r, hr_s, hl_s, h_r, hx_s, hx_r, p_s, p_r, kv_s, kv_r,
    qc_s, qc_r, qy_s, qy_r, g_s, g_r, gx_s, gx_r, fc_s, fc_r, f_s, f_r,
):
    S, D, T = sizes
    Y = D // CORES
    s, d, t = lax.axis_index("section"), lax.axis_index("dp"), lax.axis_index("tensor")
    y, c = d // CORES, d % CORES
    sibling = y * CORES + 1 - c
    rows = image.shape[0]
    image_count = S * rows
    kc = key_w.shape[1]
    width = wq.shape[1]
    feats = wq.shape[0]
    heads_here = kc // HEAD_SIZE
    pair = 2 * HEAD_SIZE
    span = QUERY_GROUP * HEAD_SIZE
    tokens = bias.shape[0]
    part_rows = tokens // HALVES
    part_columns = feats // COLUMN_PARTS
    part_feats = feats // GRAD_PARTS
    waits = []

    def load_copy(i, src, dst):
        copy = pltpu.make_async_copy(src, dst, load.at[i])
        copy.start()
        return copy

    own_rows = pl.ds(pl.multiple_of(d * image_count + s * rows, rows), rows)
    load_image = load_copy(0, image, img.at[own_rows])
    load_hidden = [
        load_copy(
            4 + 2 * heads_here + h, hidden.at[pl.ds(h * part_rows, part_rows)], hb.at[h, t]
        )
        for h in range(HALVES)
    ]
    load_bias = load_copy(1, bias_in, bias)
    load_query = load_copy(2, w_query, wq)
    load_cot = load_copy(3, cotangent, cot)
    load_pairs = []
    for k in range(heads_here):
        head = pl.ds(k * HEAD_SIZE, HEAD_SIZE)
        load_pairs += [
            load_copy(4 + 2 * k, key_w.at[:, head], wkv.at[:, pl.ds(k * pair, HEAD_SIZE)]),
            load_copy(
                5 + 2 * k, value_w.at[:, head], wkv.at[:, pl.ds(k * pair + HEAD_SIZE, HEAD_SIZE)]
            ),
        ]

    others = [{"dp": lax.rem(d + j, D)} for j in range(1, D)]
    others += [{"tensor": lax.rem(t + j, T)} for j in range(1, T)]
    for i in range(1, S):
        for j in range(Y):
            others.append(
                {"section": lax.rem(s + i, S), "dp": lax.rem(y + j, Y) * CORES + c}
            )
    barrier = pltpu.get_barrier_semaphore()
    for device in others:
        pl.semaphore_signal(
            barrier, inc=1, device_id=device, device_id_type=pl.DeviceIdType.MESH
        )
    pl.semaphore_wait(barrier, len(others))

    load_image.wait()
    for i in range(1, S):
        to = lax.rem(s + i, S)
        copy = remote(
            img.at[own_rows], img.at[own_rows], ix_s.at[to], ix_r.at[s], {"section": to}
        )
        copy.start()
        waits.append(copy.wait_send)

    for load_half in load_hidden:
        load_half.wait()

    def piece(f, p):
        columns = pl.ds(p % COLUMN_PARTS * part_columns, part_columns)
        return hb.at[p // COLUMN_PARTS, f, :, columns]

    def right(f, h):
        return remote(piece(f, h), piece(f, h), hr_s.at[f, h], h_r.at[f, h], {"tensor": t + 1})

    def left(f, h):
        return remote(piece(f, h), piece(f, h), hl_s.at[f, h], h_r.at[f, h], {"tensor": t - 1})

    def across(f, h):
        return remote(piece(f, h), piece(T + d, h), hx_s.at[f, h], hx_r.at[d, h], {"dp": f})

    def hidden_arrive(k, h):
        pl.when(t - k >= 0)(lambda: right(t - k, h).wait_recv())
        pl.when(t + k < T)(lambda: left(t + k, h).wait_recv())

    def hidden_pass(k, h):
        if k < T - 1:
            pl.when((t - k >= 0) & (t + 1 < T))(lambda: right(t - k, h).start())
            pl.when((t + k < T) & (t >= 1))(lambda: left(t + k, h).start())
        if k:
            pl.when((t - k >= 0) & (t - k != d))(lambda: across(t - k, h).start())
            pl.when((t + k < T) & (t + k != d))(lambda: across(t + k, h).start())

    def hidden_step(k, h):
        hidden_arrive(k, h)
        hidden_pass(k, h)

    def half(h):
        return range(h * COLUMN_PARTS, (h + 1) * COLUMN_PARTS)

    def own_across(h):
        for p in half(h):
            pl.when(t != d)(lambda: across(t, p).start())

    for p in half(0):
        hidden_pass(0, p)

    def image_block(n):
        return img.at[pl.ds(pl.multiple_of(n * image_count, image_count), image_count)]

    for i in range(1, S):
        src = lax.rem(s + i, S)
        block = img.at[pl.ds(pl.multiple_of(d * image_count + src * rows, rows), rows)]
        remote(block, block, ix_s.at[src], ix_r.at[src], {"section": src}).wait_recv()
    for j in range(1, Y):
        to = lax.rem(y + j, Y)
        copy = remote(
            image_block(d), image_block(d), iy_s.at[to], iy_r.at[y], {"dp": to * CORES + c}
        )
        copy.start()
        waits.append(copy.wait_send)

    def to_sibling(n, slot):
        copy = remote(image_block(n), image_block(n), ic_s.at[slot], ic_r.at[slot], {"dp": sibling})
        copy.start()
        waits.append(copy.wait_send)

    to_sibling(d, y)
    own_across(0)
    for k in range(1, T - 1):
        for p in half(0):
            hidden_step(k, p)
    for h in range(1, HALVES):
        for p in half(h):
            hidden_pass(0, p)
        own_across(h)
    for j in range(1, Y):
        src = lax.rem(y + j, Y)
        n = src * CORES + c
        remote(
            image_block(n), image_block(n), iy_s.at[src], iy_r.at[src], {"dp": n}
        ).wait_recv()
        to_sibling(n, src)

    for p in half(0):
        hidden_step(T - 1, p)
    for p in half(1):
        hidden_step(1, p)
    for j in range(Y):
        n = j * CORES + 1 - c
        remote(
            image_block(n), image_block(n), ic_s.at[j], ic_r.at[j], {"dp": sibling}
        ).wait_recv()
    for load_pair in load_pairs:
        load_pair.wait()
    ptile = min(256, 2 * kc)

    @pl.loop(0, 2 * kc // ptile)
    def _(i):
        columns = pl.ds(pl.multiple_of(i * ptile, ptile), ptile)
        part = jnp.dot(img[...], wkv[:, columns], preferred_element_type=F32).astype(BF16)
        for n in range(D):
            pb[n, :, columns] = part[n * image_count : (n + 1) * image_count]

    for j in range(1, D):
        n = lax.rem(d + j, D)
        copy = remote(pb.at[n], pb.at[D + d], p_s.at[n], p_r.at[d], {"dp": n})
        copy.start()
        waits.append(copy.wait_send)

    for k in range(2, T - 1):
        for p in half(1):
            hidden_step(k, p)

    load_query.wait()

    def wait_tokens(n, h):
        for p in half(h):
            remote(
                piece(0, p), piece(T + n, p), hx_s.at[0, p], hx_r.at[n, p], {"dp": n}
            ).wait_recv()

    def project(block, k):
        columns = slice(k * span, (k + 1) * span)
        return jnp.dot(block, wq[:, columns], preferred_element_type=F32)

    def query_to_sibling(yy, h, k):
        return remote(
            qsib.at[yy, h, k], qsr.at[yy, h, k], qc_s.at[yy, h, k], qc_r.at[yy, h, k],
            {"dp": sibling},
        )

    def query_to_chip(yy, h, k, slot):
        return remote(
            qsend.at[yy, h, k], qr.at[slot, h, k], qy_s.at[yy, h, k], qy_r.at[slot, h, k],
            {"dp": yy * CORES + c},
        )

    def queries(h):
        wait_tokens(sibling, h)
        block = jnp.concatenate([hb[h, T + sibling], hb[h, d]], axis=0)
        for k in range(heads_here):
            part = project(block, k)
            qsib[y, h, k] = part[:part_rows].astype(BF16)
            query_to_sibling(y, h, k).start()
            waits.append(query_to_sibling(y, h, k).wait_send)
            qacc[h, k] = part[part_rows:]
        for j in range(1, Y):
            yy = lax.rem(y + j, Y)
            for core in range(CORES):
                wait_tokens(yy * CORES + core, h)
            block = hb[h, pl.ds(T + yy * CORES, CORES)].reshape(CORES * part_rows, feats)
            for k in range(heads_here):
                qfull[k] = project(block, k).reshape(CORES, part_rows, span)
                qsib[yy, h, k] = qfull[k, 1 - c].astype(BF16)
                query_to_sibling(yy, h, k).start()
                waits.append(query_to_sibling(yy, h, k).wait_send)
            for k in range(heads_here):
                query_to_sibling(yy, h, k).wait_recv()
                qsend[yy, h, k] = (qfull[k, c] + qsr[yy, h, k].astype(F32)).astype(BF16)
                query_to_chip(yy, h, k, y).start()
                waits.append(query_to_chip(yy, h, k, y).wait_send)

    queries(0)
    for p in half(1):
        hidden_step(T - 1, p)

    for j in range(1, D):
        n = lax.rem(d + j, D)
        remote(pb.at[n], pb.at[D + n], p_s.at[n], p_r.at[n], {"dp": n}).wait_recv()
    for j in range(1, T):
        f = lax.rem(t + j, T)
        copy = remote(
            pb.at[jnp.where(f == d, f, D + f)], kvr.at[t], kv_s.at[f], kv_r.at[t], {"tensor": f}
        )
        copy.start()
        waits.append(copy.wait_send)

    queries(1)
    load_cot.wait()
    load_bias.wait()
    total = pb[jnp.where(t == d, t, D + t)].astype(F32)
    for j in range(1, T):
        f = lax.rem(t + j, T)
        remote(kvr.at[f], kvr.at[f], kv_s.at[f], kv_r.at[f], {"tensor": f}).wait_recv()
        total = total + kvr[f].astype(F32)
    kvs[...] = total.astype(BF16)

    scaling = HEAD_SIZE ** (-0.5)

    def grad_piece(f, k):
        return gb.at[f, :, pl.ds(k * pair, pair)]

    def grad_along(f, k, slot, to):
        return remote(
            grad_piece(slot, k), grad_piece(slot, k), g_s.at[f, k], g_r.at[slot, k], {"tensor": to}
        )

    def grad_across(f, k):
        return remote(
            grad_piece(f, k), grad_piece(T + d, k), gx_s.at[f, k], gx_r.at[d, k], {"dp": f}
        )

    scale = jnp.tanh(jnp.full((1, HEAD_SIZE), gate[0], F32))

    def heads_on_rows(block):
        return jnp.concatenate(
            [block[:, g * HEAD_SIZE : (g + 1) * HEAD_SIZE] for g in range(QUERY_GROUP)], axis=0
        )

    def attend(h, k):
        value = kvs[:, k * pair + HEAD_SIZE : (k + 1) * pair]
        attended = scale * jnp.dot(lows[k], value, preferred_element_type=F32)
        for g in range(QUERY_GROUP):
            first = k * span + g * HEAD_SIZE
            out[h * part_rows : (h + 1) * part_rows, first : first + HEAD_SIZE] = attended[
                g * part_rows : (g + 1) * part_rows
            ].astype(BF16)

    def attention(h, k):
        half_rows = slice(h * part_rows, (h + 1) * part_rows)
        key = kvs[:, k * pair : k * pair + HEAD_SIZE]
        value = kvs[:, k * pair + HEAD_SIZE : (k + 1) * pair]
        above = heads_on_rows(cot[half_rows, k * span : (k + 1) * span])
        above = (scale * above.astype(F32)).astype(BF16)
        grad_weights = lax.dot_general(above, value, NT, preferred_element_type=F32)
        bias_rows = jnp.concatenate([bias[half_rows, :]] * QUERY_GROUP, axis=0)
        query_to_sibling(y, h, k).wait_recv()
        query = qacc[h, k] + qsr[y, h, k].astype(F32)
        for j in range(1, Y):
            yy = lax.rem(y + j, Y)
            query_to_chip(yy, h, k, yy).wait_recv()
            query = query + qr[yy, h, k].astype(F32)
        stacked = heads_on_rows(query.astype(BF16))
        scores = lax.dot_general(stacked, key, NT, preferred_element_type=F32) * scaling
        scores = scores + bias_rows
        exponent = jnp.exp(scores - jnp.max(scores, axis=-1, keepdims=True))
        weights = exponent / jnp.sum(exponent, axis=-1, keepdims=True)
        low = weights.astype(BF16)
        lows[k] = low
        value_grad = lax.dot_general(low, above, TN, preferred_element_type=F32)
        mean = jnp.sum(weights * grad_weights, axis=-1, keepdims=True)
        grad_low = (weights * (grad_weights - mean)).astype(BF16)
        key_grad = lax.dot_general(grad_low, stacked, TN, preferred_element_type=F32)
        return key_grad, value_grad

    for h in range(HALVES):
        last = h == HALVES - 1
        for k in range(heads_here):
            key_grad, value_grad = attention(h, k)
            if h:
                key_grad = key_grad + gacc[k, 0]
                value_grad = value_grad + gacc[k, 1]
            if not last:
                gacc[k, 0] = key_grad
                gacc[k, 1] = value_grad
                attend(h, k)
                continue
            gb[t, :, k * pair : k * pair + HEAD_SIZE] = (key_grad * scaling).astype(BF16)
            gb[t, :, k * pair + HEAD_SIZE : (k + 1) * pair] = value_grad.astype(BF16)
            for j in range(1, T):
                f = lax.rem(t + j, T)
                grad_along(f, k, t, f).start()
                waits.append(grad_along(f, k, t, f).wait_send)
            pl.when(t != d)(lambda: grad_across(t, k).start())
    for k in range(heads_here):
        attend(HALVES - 1, k)

    def grad_arrive(f, k):
        grad_along(f, k, f, f).wait_recv()
        pl.when(f != d)(lambda: grad_across(f, k).start())

    for k in range(heads_here):
        for i in range(1, T):
            pl.when(t - i >= 0)(functools.partial(grad_arrive, t - i, k))
            pl.when(t + i < T)(functools.partial(grad_arrive, t + i, k))

    def wait_grads(n):
        for k in range(heads_here):
            remote(
                grad_piece(0, k), grad_piece(T + n, k), gx_s.at[0, k], gx_r.at[n, k], {"dp": n}
            ).wait_recv()

    def back(block, h):
        weights_part = wkv[h * part_feats : (h + 1) * part_feats, :]
        return lax.dot_general(block, weights_part, NT, preferred_element_type=F32)

    def image_to_sibling(yy, h):
        return remote(
            fsib.at[yy, h], fsr.at[yy, h], fc_s.at[yy, h], fc_r.at[yy, h], {"dp": sibling}
        )

    def image_to_owner(yy, ss, h, slot_y, slot_s):
        return remote(
            fsend.at[yy, ss, h], fr.at[slot_y, slot_s, h],
            f_s.at[yy, ss, h], f_r.at[slot_y, slot_s, h],
            {"section": ss, "dp": yy * CORES + c},
        )

    order = list(range(1, Y)) + [0]
    sections = list(range(1, S)) + [0]
    for j in order:
        yy = lax.rem(y + j, Y)
        if j:
            for core in range(CORES):
                wait_grads(yy * CORES + core)
            block = gb[pl.ds(T + yy * CORES, CORES)].reshape(CORES * image_count, 2 * kc)
            given, kept = 1 - c, c
        else:
            wait_grads(sibling)
            block = jnp.concatenate([gb[T + sibling], gb[d]], axis=0)
            given, kept = 0, 1
        for h in range(GRAD_PARTS):
            ffull[h] = back(block, h).reshape(CORES, image_count, part_feats)
            fsib[yy, h] = ffull[h, given].astype(BF16)
            image_to_sibling(yy, h).start()
            waits.append(image_to_sibling(yy, h).wait_send)
        for h in range(GRAD_PARTS):
            image_to_sibling(yy, h).wait_recv()
            fsum[...] = ffull[h, kept] + fsr[yy, h].astype(F32)
            for i in sections:
                ss = lax.rem(s + i, S)
                mine = fsum[pl.ds(pl.multiple_of(ss * rows, rows), rows), :]
                if i == 0 and j == 0:
                    grad[:, h * part_feats : (h + 1) * part_feats] = mine
                    continue
                fsend[yy, ss, h] = mine.astype(BF16)
                image_to_owner(yy, ss, h, y, s).start()
                waits.append(image_to_owner(yy, ss, h, y, s).wait_send)
    for h in range(GRAD_PARTS):
        columns = slice(h * part_feats, (h + 1) * part_feats)
        result = grad[:, columns]
        for j in order:
            yy = lax.rem(y + j, Y)
            for i in sections:
                if i == 0 and j == 0:
                    continue
                ss = lax.rem(s + i, S)
                image_to_owner(yy, ss, h, yy, ss).wait_recv()
                result = result + fr[yy, ss, h].astype(F32)
        grad[:, columns] = result

    for wait in waits:
        wait()
    for h in range(PIECES):
        for k in range(T - 1):
            pl.when((t - k >= 0) & (t + 1 < T))(lambda: right(t - k, h).wait_send())
            pl.when((t + k < T) & (t >= 1))(lambda: left(t + k, h).wait_send())
        for f in range(T):
            pl.when(f != d)(lambda: across(f, h).wait_send())
    for k in range(heads_here):
        for f in range(T):
            pl.when(f != d)(lambda: grad_across(f, k).wait_send())


def finish(out, grad, out_result, grad_result, sems):
    copies = [
        pltpu.make_async_copy(out, out_result, sems.at[0]),
        pltpu.make_async_copy(grad, grad_result, sems.at[1]),
    ]
    for copy in copies:
        copy.start()
    for copy in copies:
        copy.wait()


def local(sizes, hidden, w_query, key_w, value_w, image, bias, gate, cotangent):
    S, D, T = sizes
    Y = D // CORES
    tokens, feats = hidden.shape[1:]
    width = w_query.shape[2]
    kc = key_w.shape[2]
    rows = image.shape[1]
    images = S * rows
    heads = kc // HEAD_SIZE
    span = QUERY_GROUP * HEAD_SIZE
    part_rows = tokens // HALVES
    part_feats = feats // GRAD_PARTS
    sem = lambda *n: pltpu.SemaphoreType.DMA(n)
    hbm = pl.BlockSpec(memory_space=pl.ANY)
    vmem = pl.BlockSpec(memory_space=pltpu.VMEM)
    smem = pl.BlockSpec(memory_space=pltpu.SMEM)
    out, grad = pl.pallas_call(
        functools.partial(kernel, sizes),
        out_shape=(
            jax.ShapeDtypeStruct((tokens, width), BF16),
            jax.ShapeDtypeStruct((rows, feats), F32),
        ),
        in_specs=[hbm] * 6 + [smem, hbm],
        out_specs=(vmem, vmem),
        scratch_shapes=[
            pltpu.VMEM((tokens, images), F32),
            pltpu.VMEM((feats, width), BF16),
            pltpu.VMEM((feats, 2 * kc), BF16),
            pltpu.VMEM((D * images, feats), BF16),
            pltpu.VMEM((tokens, width), BF16),
            pltpu.VMEM((HALVES, T + D, part_rows, feats), BF16),
            pltpu.VMEM((2 * D, images, 2 * kc), BF16),
            pltpu.VMEM((T, images, 2 * kc), BF16),
            pltpu.VMEM((images, 2 * kc), BF16),
            pltpu.VMEM((Y, HALVES, heads, part_rows, span), BF16),
            pltpu.VMEM((Y, HALVES, heads, part_rows, span), BF16),
            pltpu.VMEM((Y, HALVES, heads, part_rows, span), BF16),
            pltpu.VMEM((Y, HALVES, heads, part_rows, span), BF16),
            pltpu.VMEM((heads, CORES, part_rows, span), F32),
            pltpu.VMEM((HALVES, heads, part_rows, span), F32),
            pltpu.VMEM((heads, QUERY_GROUP * part_rows, images), BF16),
            pltpu.VMEM((heads, 2, images, HEAD_SIZE), F32),
            pltpu.VMEM((T + D, images, 2 * kc), BF16),
            pltpu.VMEM((Y, GRAD_PARTS, images, part_feats), BF16),
            pltpu.VMEM((Y, GRAD_PARTS, images, part_feats), BF16),
            pltpu.VMEM((GRAD_PARTS, CORES, images, part_feats), F32),
            pltpu.VMEM((images, part_feats), F32),
            pltpu.VMEM((Y, S, GRAD_PARTS, rows, part_feats), BF16),
            pltpu.VMEM((Y, S, GRAD_PARTS, rows, part_feats), BF16),
            sem(4 + 2 * heads + HALVES),
            sem(S), sem(S), sem(Y), sem(Y), sem(Y), sem(Y),
            sem(T, PIECES), sem(T, PIECES), sem(T, PIECES), sem(T, PIECES), sem(D, PIECES),
            sem(D), sem(D), sem(T), sem(T),
            sem(Y, HALVES, heads), sem(Y, HALVES, heads),
            sem(Y, HALVES, heads), sem(Y, HALVES, heads),
            sem(T, heads), sem(T, heads), sem(T, heads), sem(D, heads),
            sem(Y, GRAD_PARTS), sem(Y, GRAD_PARTS),
            sem(Y, S, GRAD_PARTS), sem(Y, S, GRAD_PARTS),
        ],
        compiler_params=pltpu.CompilerParams(
            collective_id=0, has_side_effects=True, vmem_limit_bytes=VMEM_BYTES
        ),
    )(hidden[0], w_query[0], key_w[0], value_w[0], image[0], bias, gate, cotangent[0])
    out, grad = pl.pallas_call(
        finish,
        out_shape=(
            jax.ShapeDtypeStruct((tokens, width), BF16),
            jax.ShapeDtypeStruct((rows, feats), F32),
        ),
        in_specs=[hbm, hbm],
        out_specs=(hbm, hbm),
        scratch_shapes=[sem(2)],
        compiler_params=pltpu.CompilerParams(vmem_limit_bytes=VMEM_BYTES),
    )(out, grad)
    return out[None], grad[None]


def solution(mesh):
    sizes = tuple(mesh.shape[name] for name in ("section", "dp", "tensor"))
    assert sizes[1] == sizes[2] and sizes[1] % CORES == 0
    in_specs = (
        P("section", "dp", "tensor"),
        P("section", "dp", "tensor"),
        P("section", "tensor", "dp"),
        P("section", "tensor", "dp"),
        P("dp", "section", "tensor"),
        P("dp", None),
        P("section"),
        P("section", "dp", "tensor"),
    )
    out_specs = (P("section", "dp", "tensor"), P("dp", "section", "tensor"))
    return jax.shard_map(
        functools.partial(local, sizes),
        mesh=mesh, in_specs=in_specs, out_specs=out_specs, check_vma=False,
    )
```

```python
import functools

import jax
import jax.numpy as jnp
from jax import lax
from jax.experimental import pallas as pl
from jax.experimental.pallas import tpu as pltpu
from jax.sharding import PartitionSpec as P

HEAD_SIZE = 128
QUERY_GROUP = 4
VMEM_BYTES = 64 * 1024 * 1024 - 64 * 1024
HALVES = 2
COLUMN_PARTS = 2
PIECES = HALVES * COLUMN_PARTS
GRAD_PARTS = 2
CORES = 2
BF16 = jnp.bfloat16
F32 = jnp.float32
NT = (((1,), (1,)), ((), ()))
TN = (((0,), (0,)), ((), ()))


def remote(src, dst, send_sem, recv_sem, device):
    return pltpu.make_async_remote_copy(
        src_ref=src,
        dst_ref=dst,
        send_sem=send_sem,
        recv_sem=recv_sem,
        device_id=device,
        device_id_type=pl.DeviceIdType.MESH,
    )


def kernel(
    sizes, hidden, w_query, key_w, value_w, image, bias_in, gate, cotangent, out, grad,
    bias, wq, wkv, wkvt, img, cot, hb, pb, kvr, kvs, qsib, qsr, qsend, qr, qfull, qacc, above, wgrad, lows, gacc, gb, fsib, fsr, ffull, fsum, fsend, fr,
    load, ix_s, ix_r, iy_s, iy_r, ic_s, ic_r, hr_s, hl_s, h_r, hx_s, hx_r, p_s, p_r, kv_s, kv_r,
    qc_s, qc_r, qy_s, qy_r, g_s, g_r, gx_s, gx_r, fc_s, fc_r, f_s, f_r,
):
    S, D, T = sizes
    Y = D // CORES
    s, d, t = lax.axis_index("section"), lax.axis_index("dp"), lax.axis_index("tensor")
    y, c = d // CORES, d % CORES
    sibling = y * CORES + 1 - c
    rows = image.shape[0]
    image_count = S * rows
    kc = key_w.shape[1]
    width = wq.shape[1]
    feats = wq.shape[0]
    heads_here = kc // HEAD_SIZE
    pair = 2 * HEAD_SIZE
    span = QUERY_GROUP * HEAD_SIZE
    tokens = bias.shape[0]
    part_rows = tokens // HALVES
    part_columns = feats // COLUMN_PARTS
    part_feats = feats // GRAD_PARTS
    waits = []

    def load_copy(i, src, dst):
        copy = pltpu.make_async_copy(src, dst, load.at[i])
        copy.start()
        return copy

    own_rows = pl.ds(pl.multiple_of(d * image_count + s * rows, rows), rows)
    load_image = load_copy(0, image, img.at[own_rows])
    load_hidden = [
        load_copy(
            4 + 2 * heads_here + h, hidden.at[pl.ds(h * part_rows, part_rows)], hb.at[h, t]
        )
        for h in range(HALVES)
    ]
    load_bias = load_copy(1, bias_in, bias)
    load_query = load_copy(2, w_query, wq)
    load_cot = load_copy(3, cotangent, cot)
    load_pairs = []
    for k in range(heads_here):
        head = pl.ds(k * HEAD_SIZE, HEAD_SIZE)
        load_pairs += [
            load_copy(4 + 2 * k, key_w.at[:, head], wkv.at[:, pl.ds(k * pair, HEAD_SIZE)]),
            load_copy(
                5 + 2 * k, value_w.at[:, head], wkv.at[:, pl.ds(k * pair + HEAD_SIZE, HEAD_SIZE)]
            ),
        ]

    others = [{"dp": lax.rem(d + j, D)} for j in range(1, D)]
    others += [{"tensor": lax.rem(t + j, T)} for j in range(1, T)]
    for i in range(1, S):
        for j in range(Y):
            others.append(
                {"section": lax.rem(s + i, S), "dp": lax.rem(y + j, Y) * CORES + c}
            )
    barrier = pltpu.get_barrier_semaphore()
    for device in others:
        pl.semaphore_signal(
            barrier, inc=1, device_id=device, device_id_type=pl.DeviceIdType.MESH
        )
    pl.semaphore_wait(barrier, len(others))

    load_image.wait()
    for i in range(1, S):
        to = lax.rem(s + i, S)
        copy = remote(
            img.at[own_rows], img.at[own_rows], ix_s.at[to], ix_r.at[s], {"section": to}
        )
        copy.start()
        waits.append(copy.wait_send)

    for load_half in load_hidden:
        load_half.wait()

    def piece(f, p):
        columns = pl.ds(p % COLUMN_PARTS * part_columns, part_columns)
        return hb.at[p // COLUMN_PARTS, f, :, columns]

    def right(f, h):
        return remote(piece(f, h), piece(f, h), hr_s.at[f, h], h_r.at[f, h], {"tensor": t + 1})

    def left(f, h):
        return remote(piece(f, h), piece(f, h), hl_s.at[f, h], h_r.at[f, h], {"tensor": t - 1})

    def across(f, h):
        return remote(piece(f, h), piece(T + d, h), hx_s.at[f, h], hx_r.at[d, h], {"dp": f})

    def hidden_arrive(k, h):
        pl.when(t - k >= 0)(lambda: right(t - k, h).wait_recv())
        pl.when(t + k < T)(lambda: left(t + k, h).wait_recv())

    def hidden_pass(k, h):
        if k < T - 1:
            pl.when((t - k >= 0) & (t + 1 < T))(lambda: right(t - k, h).start())
            pl.when((t + k < T) & (t >= 1))(lambda: left(t + k, h).start())
        if k:
            pl.when((t - k >= 0) & (t - k != d))(lambda: across(t - k, h).start())
            pl.when((t + k < T) & (t + k != d))(lambda: across(t + k, h).start())

    def hidden_step(k, h):
        hidden_arrive(k, h)
        hidden_pass(k, h)

    def half(h):
        return range(h * COLUMN_PARTS, (h + 1) * COLUMN_PARTS)

    def own_across(h):
        for p in half(h):
            pl.when(t != d)(lambda: across(t, p).start())

    for p in half(0):
        hidden_pass(0, p)

    def image_block(n):
        return img.at[pl.ds(pl.multiple_of(n * image_count, image_count), image_count)]

    for i in range(1, S):
        src = lax.rem(s + i, S)
        block = img.at[pl.ds(pl.multiple_of(d * image_count + src * rows, rows), rows)]
        remote(block, block, ix_s.at[src], ix_r.at[src], {"section": src}).wait_recv()
    for j in range(1, Y):
        to = lax.rem(y + j, Y)
        copy = remote(
            image_block(d), image_block(d), iy_s.at[to], iy_r.at[y], {"dp": to * CORES + c}
        )
        copy.start()
        waits.append(copy.wait_send)

    def to_sibling(n, slot):
        copy = remote(image_block(n), image_block(n), ic_s.at[slot], ic_r.at[slot], {"dp": sibling})
        copy.start()
        waits.append(copy.wait_send)

    to_sibling(d, y)
    own_across(0)
    for k in range(1, T - 1):
        for p in half(0):
            hidden_step(k, p)
    for h in range(1, HALVES):
        for p in half(h):
            hidden_pass(0, p)
        own_across(h)
    for load_pair in load_pairs:
        load_pair.wait()
    for i in range(0, feats, 2 * kc):
        wkvt[:, i : i + 2 * kc] = wkv[i : i + 2 * kc, :].T
    for j in range(1, Y):
        src = lax.rem(y + j, Y)
        n = src * CORES + c
        remote(
            image_block(n), image_block(n), iy_s.at[src], iy_r.at[src], {"dp": n}
        ).wait_recv()
        to_sibling(n, src)

    for p in half(0):
        hidden_step(T - 1, p)
    for p in half(1):
        hidden_step(1, p)
    for j in range(Y):
        n = j * CORES + 1 - c
        remote(
            image_block(n), image_block(n), ic_s.at[j], ic_r.at[j], {"dp": sibling}
        ).wait_recv()
    ptile = min(256, 2 * kc)

    @pl.loop(0, 2 * kc // ptile)
    def _(i):
        columns = pl.ds(pl.multiple_of(i * ptile, ptile), ptile)
        part = jnp.dot(img[...], wkv[:, columns], preferred_element_type=F32).astype(BF16)
        for n in range(D):
            pb[n, :, columns] = part[n * image_count : (n + 1) * image_count]

    for j in range(1, D):
        n = lax.rem(d + j, D)
        copy = remote(pb.at[n], pb.at[D + d], p_s.at[n], p_r.at[d], {"dp": n})
        copy.start()
        waits.append(copy.wait_send)

    for k in range(2, T - 1):
        for p in half(1):
            hidden_step(k, p)

    load_query.wait()

    def wait_tokens(n, h):
        for p in half(h):
            remote(
                piece(0, p), piece(T + n, p), hx_s.at[0, p], hx_r.at[n, p], {"dp": n}
            ).wait_recv()

    def project(block, k):
        columns = slice(k * span, (k + 1) * span)
        return jnp.dot(block, wq[:, columns], preferred_element_type=F32)

    def query_to_sibling(yy, h, k):
        return remote(
            qsib.at[yy, h, k], qsr.at[yy, h, k], qc_s.at[yy, h, k], qc_r.at[yy, h, k],
            {"dp": sibling},
        )

    def query_to_chip(yy, h, k, slot):
        return remote(
            qsend.at[yy, h, k], qr.at[slot, h, k], qy_s.at[yy, h, k], qy_r.at[slot, h, k],
            {"dp": yy * CORES + c},
        )

    def queries(h):
        wait_tokens(sibling, h)
        block = jnp.concatenate([hb[h, T + sibling], hb[h, d]], axis=0)
        for k in range(heads_here):
            part = project(block, k)
            qsib[y, h, k] = part[:part_rows].astype(BF16)
            query_to_sibling(y, h, k).start()
            waits.append(query_to_sibling(y, h, k).wait_send)
            qacc[h, k] = part[part_rows:]
        for j in range(1, Y):
            yy = lax.rem(y + j, Y)
            for core in range(CORES):
                wait_tokens(yy * CORES + core, h)
            block = hb[h, pl.ds(T + yy * CORES, CORES)].reshape(CORES * part_rows, feats)
            for k in range(heads_here):
                qfull[k] = project(block, k).reshape(CORES, part_rows, span)
                qsib[yy, h, k] = qfull[k, 1 - c].astype(BF16)
                query_to_sibling(yy, h, k).start()
                waits.append(query_to_sibling(yy, h, k).wait_send)
            for k in range(heads_here):
                query_to_sibling(yy, h, k).wait_recv()
                qsend[yy, h, k] = (qfull[k, c] + qsr[yy, h, k].astype(F32)).astype(BF16)
                query_to_chip(yy, h, k, y).start()
                waits.append(query_to_chip(yy, h, k, y).wait_send)

    for j in range(1, D):
        n = lax.rem(d + j, D)
        remote(pb.at[n], pb.at[D + n], p_s.at[n], p_r.at[n], {"dp": n}).wait_recv()

    def pairs_to(f):
        return remote(
            pb.at[jnp.where(f == d, f, D + f)], kvr.at[t], kv_s.at[f], kv_r.at[t], {"tensor": f}
        )

    for f in range(1, T - 1):
        pl.when(t != f)(lambda: pairs_to(f).start())
    load_cot.wait()
    load_bias.wait()
    scale = jnp.tanh(jnp.full((1, HEAD_SIZE), gate[0], F32))
    queries(0)
    for f in (0, T - 1):
        pl.when(t != f)(lambda: pairs_to(f).start())

    def heads_on_rows(block):
        return jnp.concatenate(
            [block[:, g * HEAD_SIZE : (g + 1) * HEAD_SIZE] for g in range(QUERY_GROUP)], axis=0
        )

    for h in range(HALVES):
        for k in range(heads_here):
            rows_here = cot[h * part_rows : (h + 1) * part_rows, k * span : (k + 1) * span]
            above[h, k] = (scale * heads_on_rows(rows_here).astype(F32)).astype(BF16)
    for p in half(1):
        hidden_step(T - 1, p)

    queries(1)
    total = pb[jnp.where(t == d, t, D + t)].astype(F32)
    for j in range(1, T):
        f = lax.rem(t + j, T)
        remote(kvr.at[f], kvr.at[f], kv_s.at[f], kv_r.at[f], {"tensor": f}).wait_recv()
        total = total + kvr[f].astype(F32)
    kvs[...] = total.astype(BF16)
    for h in range(HALVES):
        for k in range(heads_here):
            value = kvs[:, k * pair + HEAD_SIZE : (k + 1) * pair]
            wgrad[h, k] = lax.dot_general(above[h, k], value, NT, preferred_element_type=F32)

    scaling = HEAD_SIZE ** (-0.5)

    def grad_piece(f, k):
        return gb.at[f, :, pl.ds(k * pair, pair)]

    def grad_along(f, k, slot, to):
        return remote(
            grad_piece(slot, k), grad_piece(slot, k), g_s.at[f, k], g_r.at[slot, k], {"tensor": to}
        )

    def grad_across(f, k):
        return remote(
            grad_piece(f, k), grad_piece(T + d, k), gx_s.at[f, k], gx_r.at[d, k], {"dp": f}
        )

    def attend(h, k):
        value = kvs[:, k * pair + HEAD_SIZE : (k + 1) * pair]
        attended = scale * jnp.dot(lows[k], value, preferred_element_type=F32)
        for g in range(QUERY_GROUP):
            first = k * span + g * HEAD_SIZE
            out[h * part_rows : (h + 1) * part_rows, first : first + HEAD_SIZE] = attended[
                g * part_rows : (g + 1) * part_rows
            ].astype(BF16)

    def attention(h, k):
        half_rows = slice(h * part_rows, (h + 1) * part_rows)
        key = kvs[:, k * pair : k * pair + HEAD_SIZE]
        grad_weights = wgrad[h, k]
        bias_rows = jnp.concatenate([bias[half_rows, :]] * QUERY_GROUP, axis=0)
        query_to_sibling(y, h, k).wait_recv()
        query = qacc[h, k] + qsr[y, h, k].astype(F32)
        for j in range(1, Y):
            yy = lax.rem(y + j, Y)
            query_to_chip(yy, h, k, yy).wait_recv()
            query = query + qr[yy, h, k].astype(F32)
        stacked = heads_on_rows(query.astype(BF16))
        scores = lax.dot_general(stacked, key, NT, preferred_element_type=F32) * scaling
        scores = scores + bias_rows
        exponent = jnp.exp(scores - jnp.max(scores, axis=-1, keepdims=True))
        weights = exponent * (1.0 / jnp.sum(exponent, axis=-1, keepdims=True))
        low = weights.astype(BF16)
        lows[k] = low
        value_grad = lax.dot_general(low, above[h, k], TN, preferred_element_type=F32)
        mean = jnp.sum(weights * grad_weights, axis=-1, keepdims=True)
        grad_low = (weights * (grad_weights - mean)).astype(BF16)
        key_grad = lax.dot_general(grad_low, stacked, TN, preferred_element_type=F32)
        return key_grad, value_grad

    for h in range(HALVES):
        last = h == HALVES - 1
        for k in range(heads_here):
            key_grad, value_grad = attention(h, k)
            if h:
                key_grad = key_grad + gacc[k, 0]
                value_grad = value_grad + gacc[k, 1]
            if not last:
                gacc[k, 0] = key_grad
                gacc[k, 1] = value_grad
                attend(h, k)
                continue
            gb[t, :, k * pair : k * pair + HEAD_SIZE] = (key_grad * scaling).astype(BF16)
            gb[t, :, k * pair + HEAD_SIZE : (k + 1) * pair] = value_grad.astype(BF16)
            for j in range(1, T):
                f = lax.rem(t + j, T)
                grad_along(f, k, t, f).start()
                waits.append(grad_along(f, k, t, f).wait_send)
            pl.when(t != d)(lambda: grad_across(t, k).start())
    for k in range(heads_here):
        attend(HALVES - 1, k)

    def grad_arrive(f, k):
        grad_along(f, k, f, f).wait_recv()
        pl.when(f != d)(lambda: grad_across(f, k).start())

    for k in range(heads_here):
        for i in range(1, T):
            pl.when(t - i >= 0)(functools.partial(grad_arrive, t - i, k))
            pl.when(t + i < T)(functools.partial(grad_arrive, t + i, k))

    def wait_grads(n):
        for k in range(heads_here):
            remote(
                grad_piece(0, k), grad_piece(T + n, k), gx_s.at[0, k], gx_r.at[n, k], {"dp": n}
            ).wait_recv()

    def back(block, h):
        weights_part = wkvt[:, h * part_feats : (h + 1) * part_feats]
        return jnp.dot(block, weights_part, preferred_element_type=F32)

    def image_to_sibling(yy, h):
        return remote(
            fsib.at[yy, h], fsr.at[yy, h], fc_s.at[yy, h], fc_r.at[yy, h], {"dp": sibling}
        )

    def image_to_owner(yy, ss, h, slot_y, slot_s):
        return remote(
            fsend.at[yy, ss, h], fr.at[slot_y, slot_s, h],
            f_s.at[yy, ss, h], f_r.at[slot_y, slot_s, h],
            {"section": ss, "dp": yy * CORES + c},
        )

    order = list(range(1, Y)) + [0]
    sections = list(range(1, S)) + [0]
    for j in order:
        yy = lax.rem(y + j, Y)
        if j:
            for core in range(CORES):
                wait_grads(yy * CORES + core)
            block = gb[pl.ds(T + yy * CORES, CORES)].reshape(CORES * image_count, 2 * kc)
            given, kept = 1 - c, c
        else:
            wait_grads(sibling)
            block = jnp.concatenate([gb[T + sibling], gb[d]], axis=0)
            given, kept = 0, 1
        for h in range(GRAD_PARTS):
            ffull[h] = back(block, h).reshape(CORES, image_count, part_feats)
            fsib[yy, h] = ffull[h, given].astype(BF16)
            image_to_sibling(yy, h).start()
            waits.append(image_to_sibling(yy, h).wait_send)
        for h in range(GRAD_PARTS):
            image_to_sibling(yy, h).wait_recv()
            fsum[...] = ffull[h, kept] + fsr[yy, h].astype(F32)
            for i in sections:
                ss = lax.rem(s + i, S)
                mine = fsum[pl.ds(pl.multiple_of(ss * rows, rows), rows), :]
                if i == 0 and j == 0:
                    grad[:, h * part_feats : (h + 1) * part_feats] = mine
                    continue
                fsend[yy, ss, h] = mine.astype(BF16)
                image_to_owner(yy, ss, h, y, s).start()
                waits.append(image_to_owner(yy, ss, h, y, s).wait_send)
    for h in range(GRAD_PARTS):
        columns = slice(h * part_feats, (h + 1) * part_feats)
        result = grad[:, columns]
        for j in order:
            yy = lax.rem(y + j, Y)
            for i in sections:
                if i == 0 and j == 0:
                    continue
                ss = lax.rem(s + i, S)
                image_to_owner(yy, ss, h, yy, ss).wait_recv()
                result = result + fr[yy, ss, h].astype(F32)
        grad[:, columns] = result

    for wait in waits:
        wait()
    for h in range(PIECES):
        for k in range(T - 1):
            pl.when((t - k >= 0) & (t + 1 < T))(lambda: right(t - k, h).wait_send())
            pl.when((t + k < T) & (t >= 1))(lambda: left(t + k, h).wait_send())
        for f in range(T):
            pl.when(f != d)(lambda: across(f, h).wait_send())
    for f in range(T):
        pl.when(t != f)(lambda: pairs_to(f).wait_send())
    for k in range(heads_here):
        for f in range(T):
            pl.when(f != d)(lambda: grad_across(f, k).wait_send())


def finish(out, grad, out_result, grad_result, out_held, grad_held, sems):
    arrays = [(out, out_held, out_result), (grad, grad_held, grad_result)]
    inward, outward = [], []
    for i, (source, held, result) in enumerate(arrays):
        inward.append(pltpu.make_async_copy(source, held, sems.at[i, 0]))
        outward.append(pltpu.make_async_copy(held, result, sems.at[i, 1]))
    for copy in inward:
        copy.start()
    for first, second in zip(inward, outward):
        first.wait()
        second.start()
    for copy in outward:
        copy.wait()


def local(sizes, hidden, w_query, key_w, value_w, image, bias, gate, cotangent):
    S, D, T = sizes
    Y = D // CORES
    tokens, feats = hidden.shape[1:]
    width = w_query.shape[2]
    kc = key_w.shape[2]
    rows = image.shape[1]
    images = S * rows
    heads = kc // HEAD_SIZE
    span = QUERY_GROUP * HEAD_SIZE
    part_rows = tokens // HALVES
    part_feats = feats // GRAD_PARTS
    sem = lambda *n: pltpu.SemaphoreType.DMA(n)
    hbm = pl.BlockSpec(memory_space=pl.ANY)
    vmem = pl.BlockSpec(memory_space=pltpu.VMEM)
    smem = pl.BlockSpec(memory_space=pltpu.SMEM)
    out, grad = pl.pallas_call(
        functools.partial(kernel, sizes),
        out_shape=(
            jax.ShapeDtypeStruct((tokens, width), BF16),
            jax.ShapeDtypeStruct((rows, feats), F32),
        ),
        in_specs=[hbm] * 6 + [smem, hbm],
        out_specs=(vmem, vmem),
        scratch_shapes=[
            pltpu.VMEM((tokens, images), F32),
            pltpu.VMEM((feats, width), BF16),
            pltpu.VMEM((feats, 2 * kc), BF16),
            pltpu.VMEM((2 * kc, feats), BF16),
            pltpu.VMEM((D * images, feats), BF16),
            pltpu.VMEM((tokens, width), BF16),
            pltpu.VMEM((HALVES, T + D, part_rows, feats), BF16),
            pltpu.VMEM((2 * D, images, 2 * kc), BF16),
            pltpu.VMEM((T, images, 2 * kc), BF16),
            pltpu.VMEM((images, 2 * kc), BF16),
            pltpu.VMEM((Y, HALVES, heads, part_rows, span), BF16),
            pltpu.VMEM((Y, HALVES, heads, part_rows, span), BF16),
            pltpu.VMEM((Y, HALVES, heads, part_rows, span), BF16),
            pltpu.VMEM((Y, HALVES, heads, part_rows, span), BF16),
            pltpu.VMEM((heads, CORES, part_rows, span), F32),
            pltpu.VMEM((HALVES, heads, part_rows, span), F32),
            pltpu.VMEM((HALVES, heads, QUERY_GROUP * part_rows, HEAD_SIZE), BF16),
            pltpu.VMEM((HALVES, heads, QUERY_GROUP * part_rows, images), F32),
            pltpu.VMEM((heads, QUERY_GROUP * part_rows, images), BF16),
            pltpu.VMEM((heads, 2, images, HEAD_SIZE), F32),
            pltpu.VMEM((T + D, images, 2 * kc), BF16),
            pltpu.VMEM((Y, GRAD_PARTS, images, part_feats), BF16),
            pltpu.VMEM((Y, GRAD_PARTS, images, part_feats), BF16),
            pltpu.VMEM((GRAD_PARTS, CORES, images, part_feats), F32),
            pltpu.VMEM((images, part_feats), F32),
            pltpu.VMEM((Y, S, GRAD_PARTS, rows, part_feats), BF16),
            pltpu.VMEM((Y, S, GRAD_PARTS, rows, part_feats), BF16),
            sem(4 + 2 * heads + HALVES),
            sem(S), sem(S), sem(Y), sem(Y), sem(Y), sem(Y),
            sem(T, PIECES), sem(T, PIECES), sem(T, PIECES), sem(T, PIECES), sem(D, PIECES),
            sem(D), sem(D), sem(T), sem(T),
            sem(Y, HALVES, heads), sem(Y, HALVES, heads),
            sem(Y, HALVES, heads), sem(Y, HALVES, heads),
            sem(T, heads), sem(T, heads), sem(T, heads), sem(D, heads),
            sem(Y, GRAD_PARTS), sem(Y, GRAD_PARTS),
            sem(Y, S, GRAD_PARTS), sem(Y, S, GRAD_PARTS),
        ],
        compiler_params=pltpu.CompilerParams(
            collective_id=0, has_side_effects=True, vmem_limit_bytes=VMEM_BYTES
        ),
    )(hidden[0], w_query[0], key_w[0], value_w[0], image[0], bias, gate, cotangent[0])
    out, grad = pl.pallas_call(
        finish,
        out_shape=(
            jax.ShapeDtypeStruct((tokens, width), BF16),
            jax.ShapeDtypeStruct((rows, feats), F32),
        ),
        in_specs=[hbm, hbm],
        out_specs=(hbm, hbm),
        scratch_shapes=[
            pltpu.VMEM((tokens, width), BF16),
            pltpu.VMEM((rows, feats), F32),
            sem(2, 2),
        ],
        compiler_params=pltpu.CompilerParams(vmem_limit_bytes=VMEM_BYTES),
    )(out, grad)
    return out[None], grad[None]


def solution(mesh):
    sizes = tuple(mesh.shape[name] for name in ("section", "dp", "tensor"))
    assert sizes[1] == sizes[2] and sizes[1] % CORES == 0
    in_specs = (
        P("section", "dp", "tensor"),
        P("section", "dp", "tensor"),
        P("section", "tensor", "dp"),
        P("section", "tensor", "dp"),
        P("dp", "section", "tensor"),
        P("dp", None),
        P("section"),
        P("section", "dp", "tensor"),
    )
    out_specs = (P("section", "dp", "tensor"), P("dp", "section", "tensor"))
    return jax.shard_map(
        functools.partial(local, sizes),
        mesh=mesh, in_specs=in_specs, out_specs=out_specs, check_vma=False,
    )
```

```python
import functools

import jax
import jax.numpy as jnp
from jax import lax
from jax.experimental import pallas as pl
from jax.experimental.pallas import tpu as pltpu
from jax.sharding import PartitionSpec as P

HEAD_SIZE = 128
QUERY_GROUP = 4
VMEM_BYTES = 64 * 1024 * 1024 - 64 * 1024
HALVES = 2
COLUMN_PARTS = 2
PIECES = HALVES * COLUMN_PARTS
GRAD_PARTS = 2
CORES = 2
BF16 = jnp.bfloat16
F32 = jnp.float32
NT = (((1,), (1,)), ((), ()))
TN = (((0,), (0,)), ((), ()))


def remote(src, dst, send_sem, recv_sem, device):
    return pltpu.make_async_remote_copy(
        src_ref=src,
        dst_ref=dst,
        send_sem=send_sem,
        recv_sem=recv_sem,
        device_id=device,
        device_id_type=pl.DeviceIdType.MESH,
    )


def kernel(
    sizes, hidden, w_query, key_w, value_w, image, bias_in, gate, cotangent, out, grad,
    bias, wq, wkv, img, cot, hb, pb, kvr, kvs, qsib, qsr, qsend, qr, qfull, qacc, above, wgrad, lows, gacc, gb, fsib, fsr, ffull, fsum, fsend, fr,
    load, ix_s, ix_r, iy_s, iy_r, ic_s, ic_r, hr_s, hl_s, h_r, hx_s, hx_r, p_s, p_r, kv_s, kv_r,
    qc_s, qc_r, qy_s, qy_r, g_s, g_r, gx_s, gx_r, fc_s, fc_r, f_s, f_r,
):
    S, D, T = sizes
    Y = D // CORES
    s, d, t = lax.axis_index("section"), lax.axis_index("dp"), lax.axis_index("tensor")
    y, c = d // CORES, d % CORES
    sibling = y * CORES + 1 - c
    rows = image.shape[0]
    image_count = S * rows
    kc = key_w.shape[1]
    width = wq.shape[1]
    feats = wq.shape[0]
    heads_here = kc // HEAD_SIZE
    pair = 2 * HEAD_SIZE
    span = QUERY_GROUP * HEAD_SIZE
    tokens = bias.shape[0]
    part_rows = tokens // HALVES
    part_columns = feats // COLUMN_PARTS
    part_feats = feats // GRAD_PARTS
    waits = []

    def load_copy(i, src, dst):
        copy = pltpu.make_async_copy(src, dst, load.at[i])
        copy.start()
        return copy

    own_rows = pl.ds(pl.multiple_of(d * image_count + s * rows, rows), rows)
    load_image = load_copy(0, image, img.at[own_rows])
    load_hidden = [
        load_copy(
            4 + 2 * heads_here + h, hidden.at[pl.ds(h * part_rows, part_rows)], hb.at[h, t]
        )
        for h in range(HALVES)
    ]
    load_bias = load_copy(1, bias_in, bias)
    load_query = load_copy(2, w_query, wq)
    load_cot = load_copy(3, cotangent, cot)
    load_pairs = []
    for k in range(heads_here):
        head = pl.ds(k * HEAD_SIZE, HEAD_SIZE)
        load_pairs += [
            load_copy(4 + 2 * k, key_w.at[:, head], wkv.at[:, pl.ds(k * pair, HEAD_SIZE)]),
            load_copy(
                5 + 2 * k, value_w.at[:, head], wkv.at[:, pl.ds(k * pair + HEAD_SIZE, HEAD_SIZE)]
            ),
        ]

    others = [{"dp": lax.rem(d + j, D)} for j in range(1, D)]
    others += [{"tensor": lax.rem(t + j, T)} for j in range(1, T)]
    for i in range(1, S):
        for j in range(Y):
            others.append(
                {"section": lax.rem(s + i, S), "dp": lax.rem(y + j, Y) * CORES + c}
            )
    barrier = pltpu.get_barrier_semaphore()
    for device in others:
        pl.semaphore_signal(
            barrier, inc=1, device_id=device, device_id_type=pl.DeviceIdType.MESH
        )
    pl.semaphore_wait(barrier, len(others))

    load_image.wait()
    for i in range(1, S):
        to = lax.rem(s + i, S)
        copy = remote(
            img.at[own_rows], img.at[own_rows], ix_s.at[to], ix_r.at[s], {"section": to}
        )
        copy.start()
        waits.append(copy.wait_send)

    for load_half in load_hidden:
        load_half.wait()

    def piece(f, p):
        columns = pl.ds(p % COLUMN_PARTS * part_columns, part_columns)
        return hb.at[p // COLUMN_PARTS, f, :, columns]

    def right(f, h):
        return remote(piece(f, h), piece(f, h), hr_s.at[f, h], h_r.at[f, h], {"tensor": t + 1})

    def left(f, h):
        return remote(piece(f, h), piece(f, h), hl_s.at[f, h], h_r.at[f, h], {"tensor": t - 1})

    def across(f, h):
        return remote(piece(f, h), piece(T + d, h), hx_s.at[f, h], hx_r.at[d, h], {"dp": f})

    def hidden_arrive(k, h):
        pl.when(t - k >= 0)(lambda: right(t - k, h).wait_recv())
        pl.when(t + k < T)(lambda: left(t + k, h).wait_recv())

    def hidden_pass(k, h):
        if k < T - 1:
            pl.when((t - k >= 0) & (t + 1 < T))(lambda: right(t - k, h).start())
            pl.when((t + k < T) & (t >= 1))(lambda: left(t + k, h).start())
        if k:
            pl.when((t - k >= 0) & (t - k != d))(lambda: across(t - k, h).start())
            pl.when((t + k < T) & (t + k != d))(lambda: across(t + k, h).start())

    def hidden_step(k, h):
        hidden_arrive(k, h)
        hidden_pass(k, h)

    def half(h):
        return range(h * COLUMN_PARTS, (h + 1) * COLUMN_PARTS)

    def own_across(h):
        for p in half(h):
            pl.when(t != d)(lambda: across(t, p).start())

    for p in half(0):
        hidden_pass(0, p)

    def image_block(n):
        return img.at[pl.ds(pl.multiple_of(n * image_count, image_count), image_count)]

    for i in range(1, S):
        src = lax.rem(s + i, S)
        block = img.at[pl.ds(pl.multiple_of(d * image_count + src * rows, rows), rows)]
        remote(block, block, ix_s.at[src], ix_r.at[src], {"section": src}).wait_recv()
    for j in range(1, Y):
        to = lax.rem(y + j, Y)
        copy = remote(
            image_block(d), image_block(d), iy_s.at[to], iy_r.at[y], {"dp": to * CORES + c}
        )
        copy.start()
        waits.append(copy.wait_send)

    def to_sibling(n, slot):
        copy = remote(image_block(n), image_block(n), ic_s.at[slot], ic_r.at[slot], {"dp": sibling})
        copy.start()
        waits.append(copy.wait_send)

    to_sibling(d, y)
    own_across(0)
    for k in range(1, T - 1):
        for p in half(0):
            hidden_step(k, p)
    for p in half(1):
        hidden_pass(0, p)
    for p in half(1):
        hidden_step(1, p)
    for p in half(0):
        hidden_step(T - 1, p)
    own_across(1)
    for k in range(2, T - 1):
        for p in half(1):
            hidden_step(k, p)
    for j in range(1, Y):
        src = lax.rem(y + j, Y)
        n = src * CORES + c
        remote(
            image_block(n), image_block(n), iy_s.at[src], iy_r.at[src], {"dp": n}
        ).wait_recv()
        to_sibling(n, src)

    for j in range(Y):
        n = j * CORES + 1 - c
        remote(
            image_block(n), image_block(n), ic_s.at[j], ic_r.at[j], {"dp": sibling}
        ).wait_recv()
    for load_pair in load_pairs:
        load_pair.wait()
    ptile = min(256, 2 * kc)

    @pl.loop(0, 2 * kc // ptile)
    def _(i):
        columns = pl.ds(pl.multiple_of(i * ptile, ptile), ptile)
        part = jnp.dot(img[...], wkv[:, columns], preferred_element_type=F32).astype(BF16)
        for n in range(D):
            pb[n, :, columns] = part[n * image_count : (n + 1) * image_count]

    for j in range(1, D):
        n = lax.rem(d + j, D)
        copy = remote(pb.at[n], pb.at[D + d], p_s.at[n], p_r.at[d], {"dp": n})
        copy.start()
        waits.append(copy.wait_send)


    load_query.wait()

    def wait_tokens(n, h):
        for p in half(h):
            remote(
                piece(0, p), piece(T + n, p), hx_s.at[0, p], hx_r.at[n, p], {"dp": n}
            ).wait_recv()

    def project(block, k):
        columns = slice(k * span, (k + 1) * span)
        return jnp.dot(block, wq[:, columns], preferred_element_type=F32)

    def query_to_sibling(yy, h, k):
        return remote(
            qsib.at[yy, h, k], qsr.at[yy, h, k], qc_s.at[yy, h, k], qc_r.at[yy, h, k],
            {"dp": sibling},
        )

    def query_to_chip(yy, h, k, slot):
        return remote(
            qsend.at[yy, h, k], qr.at[slot, h, k], qy_s.at[yy, h, k], qy_r.at[slot, h, k],
            {"dp": yy * CORES + c},
        )

    def queries(h):
        wait_tokens(sibling, h)
        block = jnp.concatenate([hb[h, T + sibling], hb[h, d]], axis=0)
        for k in range(heads_here):
            part = project(block, k)
            qsib[y, h, k] = part[:part_rows].astype(BF16)
            query_to_sibling(y, h, k).start()
            waits.append(query_to_sibling(y, h, k).wait_send)
            qacc[h, k] = part[part_rows:]
        for j in range(1, Y):
            yy = lax.rem(y + j, Y)
            for core in range(CORES):
                wait_tokens(yy * CORES + core, h)
            block = hb[h, pl.ds(T + yy * CORES, CORES)].reshape(CORES * part_rows, feats)
            for k in range(heads_here):
                qfull[k] = project(block, k).reshape(CORES, part_rows, span)
                qsib[yy, h, k] = qfull[k, 1 - c].astype(BF16)
                query_to_sibling(yy, h, k).start()
                waits.append(query_to_sibling(yy, h, k).wait_send)
            for k in range(heads_here):
                query_to_sibling(yy, h, k).wait_recv()
                qsend[yy, h, k] = (qfull[k, c] + qsr[yy, h, k].astype(F32)).astype(BF16)
                query_to_chip(yy, h, k, y).start()
                waits.append(query_to_chip(yy, h, k, y).wait_send)

    queries(0)

    for j in range(1, D):
        n = lax.rem(d + j, D)
        remote(pb.at[n], pb.at[D + n], p_s.at[n], p_r.at[n], {"dp": n}).wait_recv()

    def pairs_to(f):
        return remote(
            pb.at[jnp.where(f == d, f, D + f)], kvr.at[t], kv_s.at[f], kv_r.at[t], {"tensor": f}
        )

    for f in range(1, T - 1):
        pl.when(t != f)(lambda: pairs_to(f).start())
    for p in half(1):
        hidden_step(T - 1, p)
    for f in (0, T - 1):
        pl.when(t != f)(lambda: pairs_to(f).start())
    queries(1)
    load_cot.wait()
    load_bias.wait()
    scale = jnp.tanh(jnp.full((1, HEAD_SIZE), gate[0], F32))

    def heads_on_rows(block):
        return jnp.concatenate(
            [block[:, g * HEAD_SIZE : (g + 1) * HEAD_SIZE] for g in range(QUERY_GROUP)], axis=0
        )

    for h in range(HALVES):
        for k in range(heads_here):
            rows_here = cot[h * part_rows : (h + 1) * part_rows, k * span : (k + 1) * span]
            above[h, k] = (scale * heads_on_rows(rows_here).astype(F32)).astype(BF16)

    total = pb[jnp.where(t == d, t, D + t)].astype(F32)
    for j in range(1, T):
        f = lax.rem(t + j, T)
        remote(kvr.at[f], kvr.at[f], kv_s.at[f], kv_r.at[f], {"tensor": f}).wait_recv()
        total = total + kvr[f].astype(F32)
    kvs[...] = total.astype(BF16)
    for h in range(HALVES):
        for k in range(heads_here):
            value = kvs[:, k * pair + HEAD_SIZE : (k + 1) * pair]
            wgrad[h, k] = lax.dot_general(above[h, k], value, NT, preferred_element_type=F32)

    scaling = HEAD_SIZE ** (-0.5)

    def grad_piece(f, k):
        return gb.at[f, :, pl.ds(k * pair, pair)]

    def grad_along(f, k, slot, to):
        return remote(
            grad_piece(slot, k), grad_piece(slot, k), g_s.at[f, k], g_r.at[slot, k], {"tensor": to}
        )

    def grad_across(f, k):
        return remote(
            grad_piece(f, k), grad_piece(T + d, k), gx_s.at[f, k], gx_r.at[d, k], {"dp": f}
        )

    def attend(h, k):
        value = kvs[:, k * pair + HEAD_SIZE : (k + 1) * pair]
        attended = scale * jnp.dot(lows[k], value, preferred_element_type=F32)
        for g in range(QUERY_GROUP):
            first = k * span + g * HEAD_SIZE
            out[h * part_rows : (h + 1) * part_rows, first : first + HEAD_SIZE] = attended[
                g * part_rows : (g + 1) * part_rows
            ].astype(BF16)

    def attention(h, k):
        half_rows = slice(h * part_rows, (h + 1) * part_rows)
        key = kvs[:, k * pair : k * pair + HEAD_SIZE]
        grad_weights = wgrad[h, k]
        bias_rows = jnp.concatenate([bias[half_rows, :]] * QUERY_GROUP, axis=0)
        query_to_sibling(y, h, k).wait_recv()
        query = qacc[h, k] + qsr[y, h, k].astype(F32)
        for j in range(1, Y):
            yy = lax.rem(y + j, Y)
            query_to_chip(yy, h, k, yy).wait_recv()
            query = query + qr[yy, h, k].astype(F32)
        stacked = heads_on_rows(query.astype(BF16))
        scores = lax.dot_general(stacked, key, NT, preferred_element_type=F32) * scaling
        scores = scores + bias_rows
        exponent = jnp.exp(scores - jnp.max(scores, axis=-1, keepdims=True))
        weights = exponent * (1.0 / jnp.sum(exponent, axis=-1, keepdims=True))
        low = weights.astype(BF16)
        lows[k] = low
        value_grad = lax.dot_general(low, above[h, k], TN, preferred_element_type=F32)
        mean = jnp.sum(weights * grad_weights, axis=-1, keepdims=True)
        grad_low = (weights * (grad_weights - mean)).astype(BF16)
        key_grad = lax.dot_general(grad_low, stacked, TN, preferred_element_type=F32)
        return key_grad, value_grad

    for h in range(HALVES):
        last = h == HALVES - 1
        for k in range(heads_here):
            key_grad, value_grad = attention(h, k)
            if h:
                key_grad = key_grad + gacc[k, 0]
                value_grad = value_grad + gacc[k, 1]
            if not last:
                gacc[k, 0] = key_grad
                gacc[k, 1] = value_grad
                attend(h, k)
                continue
            gb[t, :, k * pair : k * pair + HEAD_SIZE] = (key_grad * scaling).astype(BF16)
            gb[t, :, k * pair + HEAD_SIZE : (k + 1) * pair] = value_grad.astype(BF16)
            for j in range(1, T):
                f = lax.rem(t + j, T)
                grad_along(f, k, t, f).start()
                waits.append(grad_along(f, k, t, f).wait_send)
            pl.when(t != d)(lambda: grad_across(t, k).start())
    for k in range(heads_here):
        attend(HALVES - 1, k)

    def grad_arrive(f, k):
        grad_along(f, k, f, f).wait_recv()
        pl.when(f != d)(lambda: grad_across(f, k).start())

    for k in range(heads_here):
        for i in range(1, T):
            pl.when(t - i >= 0)(functools.partial(grad_arrive, t - i, k))
            pl.when(t + i < T)(functools.partial(grad_arrive, t + i, k))

    def wait_grads(n):
        for k in range(heads_here):
            remote(
                grad_piece(0, k), grad_piece(T + n, k), gx_s.at[0, k], gx_r.at[n, k], {"dp": n}
            ).wait_recv()

    def back(block, h):
        weights_part = wkv[h * part_feats : (h + 1) * part_feats, :]
        return lax.dot_general(block, weights_part, NT, preferred_element_type=F32)

    def image_to_sibling(yy, h):
        return remote(
            fsib.at[yy, h], fsr.at[yy, h], fc_s.at[yy, h], fc_r.at[yy, h], {"dp": sibling}
        )

    def image_to_owner(yy, ss, h, slot_y, slot_s):
        return remote(
            fsend.at[yy, ss, h], fr.at[slot_y, slot_s, h],
            f_s.at[yy, ss, h], f_r.at[slot_y, slot_s, h],
            {"section": ss, "dp": yy * CORES + c},
        )

    order = list(range(1, Y)) + [0]
    sections = list(range(1, S)) + [0]
    for j in order:
        yy = lax.rem(y + j, Y)
        if j:
            for core in range(CORES):
                wait_grads(yy * CORES + core)
            block = gb[pl.ds(T + yy * CORES, CORES)].reshape(CORES * image_count, 2 * kc)
            given, kept = 1 - c, c
        else:
            wait_grads(sibling)
            block = jnp.concatenate([gb[T + sibling], gb[d]], axis=0)
            given, kept = 0, 1
        for h in range(GRAD_PARTS):
            ffull[h] = back(block, h).reshape(CORES, image_count, part_feats)
            fsib[yy, h] = ffull[h, given].astype(BF16)
            image_to_sibling(yy, h).start()
            waits.append(image_to_sibling(yy, h).wait_send)
        for h in range(GRAD_PARTS):
            image_to_sibling(yy, h).wait_recv()
            fsum[...] = ffull[h, kept] + fsr[yy, h].astype(F32)
            for i in sections:
                ss = lax.rem(s + i, S)
                mine = fsum[pl.ds(pl.multiple_of(ss * rows, rows), rows), :]
                if i == 0 and j == 0:
                    grad[:, h * part_feats : (h + 1) * part_feats] = mine
                    continue
                fsend[yy, ss, h] = mine.astype(BF16)
                image_to_owner(yy, ss, h, y, s).start()
                waits.append(image_to_owner(yy, ss, h, y, s).wait_send)
    for h in range(GRAD_PARTS):
        columns = slice(h * part_feats, (h + 1) * part_feats)
        result = grad[:, columns]
        for j in order:
            yy = lax.rem(y + j, Y)
            for i in sections:
                if i == 0 and j == 0:
                    continue
                ss = lax.rem(s + i, S)
                image_to_owner(yy, ss, h, yy, ss).wait_recv()
                result = result + fr[yy, ss, h].astype(F32)
        grad[:, columns] = result

    for wait in waits:
        wait()
    for h in range(PIECES):
        for k in range(T - 1):
            pl.when((t - k >= 0) & (t + 1 < T))(lambda: right(t - k, h).wait_send())
            pl.when((t + k < T) & (t >= 1))(lambda: left(t + k, h).wait_send())
        for f in range(T):
            pl.when(f != d)(lambda: across(f, h).wait_send())
    for f in range(T):
        pl.when(t != f)(lambda: pairs_to(f).wait_send())
    for k in range(heads_here):
        for f in range(T):
            pl.when(f != d)(lambda: grad_across(f, k).wait_send())


def finish(out, grad, out_result, grad_result, out_held, grad_held, sems):
    arrays = [(out, out_held, out_result), (grad, grad_held, grad_result)]
    inward, outward = [], []
    for i, (source, held, result) in enumerate(arrays):
        inward.append(pltpu.make_async_copy(source, held, sems.at[i, 0]))
        outward.append(pltpu.make_async_copy(held, result, sems.at[i, 1]))
    for copy in inward:
        copy.start()
    for first, second in zip(inward, outward):
        first.wait()
        second.start()
    for copy in outward:
        copy.wait()


def local(sizes, hidden, w_query, key_w, value_w, image, bias, gate, cotangent):
    S, D, T = sizes
    Y = D // CORES
    tokens, feats = hidden.shape[1:]
    width = w_query.shape[2]
    kc = key_w.shape[2]
    rows = image.shape[1]
    images = S * rows
    heads = kc // HEAD_SIZE
    span = QUERY_GROUP * HEAD_SIZE
    part_rows = tokens // HALVES
    part_feats = feats // GRAD_PARTS
    sem = lambda *n: pltpu.SemaphoreType.DMA(n)
    hbm = pl.BlockSpec(memory_space=pl.ANY)
    vmem = pl.BlockSpec(memory_space=pltpu.VMEM)
    smem = pl.BlockSpec(memory_space=pltpu.SMEM)
    out, grad = pl.pallas_call(
        functools.partial(kernel, sizes),
        out_shape=(
            jax.ShapeDtypeStruct((tokens, width), BF16),
            jax.ShapeDtypeStruct((rows, feats), F32),
        ),
        in_specs=[hbm] * 6 + [smem, hbm],
        out_specs=(vmem, vmem),
        scratch_shapes=[
            pltpu.VMEM((tokens, images), F32),
            pltpu.VMEM((feats, width), BF16),
            pltpu.VMEM((feats, 2 * kc), BF16),
            pltpu.VMEM((D * images, feats), BF16),
            pltpu.VMEM((tokens, width), BF16),
            pltpu.VMEM((HALVES, T + D, part_rows, feats), BF16),
            pltpu.VMEM((2 * D, images, 2 * kc), BF16),
            pltpu.VMEM((T, images, 2 * kc), BF16),
            pltpu.VMEM((images, 2 * kc), BF16),
            pltpu.VMEM((Y, HALVES, heads, part_rows, span), BF16),
            pltpu.VMEM((Y, HALVES, heads, part_rows, span), BF16),
            pltpu.VMEM((Y, HALVES, heads, part_rows, span), BF16),
            pltpu.VMEM((Y, HALVES, heads, part_rows, span), BF16),
            pltpu.VMEM((heads, CORES, part_rows, span), F32),
            pltpu.VMEM((HALVES, heads, part_rows, span), F32),
            pltpu.VMEM((HALVES, heads, QUERY_GROUP * part_rows, HEAD_SIZE), BF16),
            pltpu.VMEM((HALVES, heads, QUERY_GROUP * part_rows, images), F32),
            pltpu.VMEM((heads, QUERY_GROUP * part_rows, images), BF16),
            pltpu.VMEM((heads, 2, images, HEAD_SIZE), F32),
            pltpu.VMEM((T + D, images, 2 * kc), BF16),
            pltpu.VMEM((Y, GRAD_PARTS, images, part_feats), BF16),
            pltpu.VMEM((Y, GRAD_PARTS, images, part_feats), BF16),
            pltpu.VMEM((GRAD_PARTS, CORES, images, part_feats), F32),
            pltpu.VMEM((images, part_feats), F32),
            pltpu.VMEM((Y, S, GRAD_PARTS, rows, part_feats), BF16),
            pltpu.VMEM((Y, S, GRAD_PARTS, rows, part_feats), BF16),
            sem(4 + 2 * heads + HALVES),
            sem(S), sem(S), sem(Y), sem(Y), sem(Y), sem(Y),
            sem(T, PIECES), sem(T, PIECES), sem(T, PIECES), sem(T, PIECES), sem(D, PIECES),
            sem(D), sem(D), sem(T), sem(T),
            sem(Y, HALVES, heads), sem(Y, HALVES, heads),
            sem(Y, HALVES, heads), sem(Y, HALVES, heads),
            sem(T, heads), sem(T, heads), sem(T, heads), sem(D, heads),
            sem(Y, GRAD_PARTS), sem(Y, GRAD_PARTS),
            sem(Y, S, GRAD_PARTS), sem(Y, S, GRAD_PARTS),
        ],
        compiler_params=pltpu.CompilerParams(
            collective_id=0, has_side_effects=True, vmem_limit_bytes=VMEM_BYTES
        ),
    )(hidden[0], w_query[0], key_w[0], value_w[0], image[0], bias, gate, cotangent[0])
    out, grad = pl.pallas_call(
        finish,
        out_shape=(
            jax.ShapeDtypeStruct((tokens, width), BF16),
            jax.ShapeDtypeStruct((rows, feats), F32),
        ),
        in_specs=[hbm, hbm],
        out_specs=(hbm, hbm),
        scratch_shapes=[
            pltpu.VMEM((tokens, width), BF16),
            pltpu.VMEM((rows, feats), F32),
            sem(2, 2),
        ],
        compiler_params=pltpu.CompilerParams(vmem_limit_bytes=VMEM_BYTES),
    )(out, grad)
    return out[None], grad[None]


def solution(mesh):
    sizes = tuple(mesh.shape[name] for name in ("section", "dp", "tensor"))
    assert sizes[1] == sizes[2] and sizes[1] % CORES == 0
    in_specs = (
        P("section", "dp", "tensor"),
        P("section", "dp", "tensor"),
        P("section", "tensor", "dp"),
        P("section", "tensor", "dp"),
        P("dp", "section", "tensor"),
        P("dp", None),
        P("section"),
        P("section", "dp", "tensor"),
    )
    out_specs = (P("section", "dp", "tensor"), P("dp", "section", "tensor"))
    return jax.shard_map(
        functools.partial(local, sizes),
        mesh=mesh, in_specs=in_specs, out_specs=out_specs, check_vma=False,
    )
```

```python
import functools

import jax
import jax.numpy as jnp
from jax import lax
from jax.experimental import pallas as pl
from jax.experimental.pallas import tpu as pltpu
from jax.sharding import PartitionSpec as P

HEAD_SIZE = 128
QUERY_GROUP = 4
VMEM_BYTES = 64 * 1024 * 1024 - 64 * 1024
HALVES = 2
COLUMN_PARTS = 2
PIECES = HALVES * COLUMN_PARTS
GRAD_PARTS = 2
CORES = 2
BF16 = jnp.bfloat16
F32 = jnp.float32
NT = (((1,), (1,)), ((), ()))
TN = (((0,), (0,)), ((), ()))


def row_parts(tokens):
    first = tokens * 3 // 5 // 16 * 16
    return (0, first), (first, tokens - first)


def remote(src, dst, send_sem, recv_sem, device):
    return pltpu.make_async_remote_copy(
        src_ref=src,
        dst_ref=dst,
        send_sem=send_sem,
        recv_sem=recv_sem,
        device_id=device,
        device_id_type=pl.DeviceIdType.MESH,
    )


def kernel(
    sizes, hidden, w_query, key_w, value_w, image, bias_in, gate, cotangent, out, grad,
    bias, wq, wkv, img, cot, hb, pb, kvr, kvs, qsib, qsr, qsend, qr, qfull, qacc, above, wgrad, lows, gacc, gb, fsib, fsr, ffull, fsum, fsend, fr,
    load, ix_s, ix_r, iy_s, iy_r, ic_s, ic_r, hr_s, hl_s, h_r, hx_s, hx_r, p_s, p_r, kv_s, kv_r,
    qc_s, qc_r, qy_s, qy_r, g_s, g_r, gx_s, gx_r, fc_s, fc_r, f_s, f_r,
):
    S, D, T = sizes
    Y = D // CORES
    s, d, t = lax.axis_index("section"), lax.axis_index("dp"), lax.axis_index("tensor")
    y, c = d // CORES, d % CORES
    sibling = y * CORES + 1 - c
    rows = image.shape[0]
    image_count = S * rows
    kc = key_w.shape[1]
    width = wq.shape[1]
    feats = wq.shape[0]
    heads_here = kc // HEAD_SIZE
    pair = 2 * HEAD_SIZE
    span = QUERY_GROUP * HEAD_SIZE
    tokens = bias.shape[0]
    parts = row_parts(tokens)
    part_columns = feats // COLUMN_PARTS
    part_feats = feats // GRAD_PARTS
    waits = []

    def load_copy(i, src, dst):
        copy = pltpu.make_async_copy(src, dst, load.at[i])
        copy.start()
        return copy

    own_rows = pl.ds(pl.multiple_of(d * image_count + s * rows, rows), rows)
    load_image = load_copy(0, image, img.at[own_rows])
    load_hidden = [
        load_copy(
            4 + 2 * heads_here + h, hidden.at[pl.ds(*parts[h])], hb.at[h, t, pl.ds(0, parts[h][1])]
        )
        for h in range(HALVES)
    ]
    load_bias = load_copy(1, bias_in, bias)
    load_query = load_copy(2, w_query, wq)
    load_cot = load_copy(3, cotangent, cot)
    load_pairs = []
    for k in range(heads_here):
        head = pl.ds(k * HEAD_SIZE, HEAD_SIZE)
        load_pairs += [
            load_copy(4 + 2 * k, key_w.at[:, head], wkv.at[:, pl.ds(k * pair, HEAD_SIZE)]),
            load_copy(
                5 + 2 * k, value_w.at[:, head], wkv.at[:, pl.ds(k * pair + HEAD_SIZE, HEAD_SIZE)]
            ),
        ]

    others = [{"dp": lax.rem(d + j, D)} for j in range(1, D)]
    others += [{"tensor": lax.rem(t + j, T)} for j in range(1, T)]
    for i in range(1, S):
        for j in range(Y):
            others.append(
                {"section": lax.rem(s + i, S), "dp": lax.rem(y + j, Y) * CORES + c}
            )
    barrier = pltpu.get_barrier_semaphore()
    for device in others:
        pl.semaphore_signal(
            barrier, inc=1, device_id=device, device_id_type=pl.DeviceIdType.MESH
        )
    pl.semaphore_wait(barrier, len(others))

    load_image.wait()
    for i in range(1, S):
        to = lax.rem(s + i, S)
        copy = remote(
            img.at[own_rows], img.at[own_rows], ix_s.at[to], ix_r.at[s], {"section": to}
        )
        copy.start()
        waits.append(copy.wait_send)

    for load_half in load_hidden:
        load_half.wait()

    def piece(f, p):
        columns = pl.ds(p % COLUMN_PARTS * part_columns, part_columns)
        h = p // COLUMN_PARTS
        return hb.at[h, f, pl.ds(0, parts[h][1]), columns]

    def right(f, h):
        return remote(piece(f, h), piece(f, h), hr_s.at[f, h], h_r.at[f, h], {"tensor": t + 1})

    def left(f, h):
        return remote(piece(f, h), piece(f, h), hl_s.at[f, h], h_r.at[f, h], {"tensor": t - 1})

    def across(f, h):
        return remote(piece(f, h), piece(T + d, h), hx_s.at[f, h], hx_r.at[d, h], {"dp": f})

    def hidden_arrive(k, h):
        pl.when(t - k >= 0)(lambda: right(t - k, h).wait_recv())
        pl.when(t + k < T)(lambda: left(t + k, h).wait_recv())

    def hidden_pass(k, h):
        if k < T - 1:
            pl.when((t - k >= 0) & (t + 1 < T))(lambda: right(t - k, h).start())
            pl.when((t + k < T) & (t >= 1))(lambda: left(t + k, h).start())
        if k:
            pl.when((t - k >= 0) & (t - k != d))(lambda: across(t - k, h).start())
            pl.when((t + k < T) & (t + k != d))(lambda: across(t + k, h).start())

    def hidden_step(k, h):
        hidden_arrive(k, h)
        hidden_pass(k, h)

    def half(h):
        return range(h * COLUMN_PARTS, (h + 1) * COLUMN_PARTS)

    def own_across(h):
        for p in half(h):
            pl.when(t != d)(lambda: across(t, p).start())

    for p in half(0):
        hidden_pass(0, p)

    def image_block(n):
        return img.at[pl.ds(pl.multiple_of(n * image_count, image_count), image_count)]

    for i in range(1, S):
        src = lax.rem(s + i, S)
        block = img.at[pl.ds(pl.multiple_of(d * image_count + src * rows, rows), rows)]
        remote(block, block, ix_s.at[src], ix_r.at[src], {"section": src}).wait_recv()
    for j in range(1, Y):
        to = lax.rem(y + j, Y)
        copy = remote(
            image_block(d), image_block(d), iy_s.at[to], iy_r.at[y], {"dp": to * CORES + c}
        )
        copy.start()
        waits.append(copy.wait_send)

    def to_sibling(n, slot):
        copy = remote(image_block(n), image_block(n), ic_s.at[slot], ic_r.at[slot], {"dp": sibling})
        copy.start()
        waits.append(copy.wait_send)

    to_sibling(d, y)
    own_across(0)
    for k in range(1, T - 1):
        for p in half(0):
            hidden_step(k, p)
    for p in half(1):
        hidden_pass(0, p)
    for p in half(1):
        hidden_step(1, p)
    for p in half(0):
        hidden_step(T - 1, p)
    own_across(1)
    for k in range(2, T - 1):
        for p in half(1):
            hidden_step(k, p)
    for j in range(1, Y):
        src = lax.rem(y + j, Y)
        n = src * CORES + c
        remote(
            image_block(n), image_block(n), iy_s.at[src], iy_r.at[src], {"dp": n}
        ).wait_recv()
        to_sibling(n, src)

    for j in range(Y):
        n = j * CORES + 1 - c
        remote(
            image_block(n), image_block(n), ic_s.at[j], ic_r.at[j], {"dp": sibling}
        ).wait_recv()
    for load_pair in load_pairs:
        load_pair.wait()
    ptile = min(256, 2 * kc)

    @pl.loop(0, 2 * kc // ptile)
    def _(i):
        columns = pl.ds(pl.multiple_of(i * ptile, ptile), ptile)
        part = jnp.dot(img[...], wkv[:, columns], preferred_element_type=F32).astype(BF16)
        for n in range(D):
            pb[n, :, columns] = part[n * image_count : (n + 1) * image_count]

    for j in range(1, D):
        n = lax.rem(d + j, D)
        copy = remote(pb.at[n], pb.at[D + d], p_s.at[n], p_r.at[d], {"dp": n})
        copy.start()
        waits.append(copy.wait_send)


    load_query.wait()

    def wait_tokens(n, h):
        for p in half(h):
            remote(
                piece(0, p), piece(T + n, p), hx_s.at[0, p], hx_r.at[n, p], {"dp": n}
            ).wait_recv()

    def project(block, k):
        columns = slice(k * span, (k + 1) * span)
        return jnp.dot(block, wq[:, columns], preferred_element_type=F32)

    def query_to_sibling(yy, h, k):
        held = pl.ds(0, parts[h][1])
        return remote(
            qsib.at[yy, h, k, held], qsr.at[yy, h, k, held], qc_s.at[yy, h, k], qc_r.at[yy, h, k],
            {"dp": sibling},
        )

    def query_to_chip(yy, h, k, slot):
        held = pl.ds(0, parts[h][1])
        return remote(
            qsend.at[yy, h, k, held], qr.at[slot, h, k, held], qy_s.at[yy, h, k], qy_r.at[slot, h, k],
            {"dp": yy * CORES + c},
        )

    def queries(h):
        count = parts[h][1]
        wait_tokens(sibling, h)
        block = jnp.concatenate([hb[h, T + sibling, :count], hb[h, d, :count]], axis=0)
        for k in range(heads_here):
            part = project(block, k)
            qsib[y, h, k, :count] = part[:count].astype(BF16)
            query_to_sibling(y, h, k).start()
            waits.append(query_to_sibling(y, h, k).wait_send)
            qacc[h, k, :count] = part[count:]
        for j in range(1, Y):
            yy = lax.rem(y + j, Y)
            for core in range(CORES):
                wait_tokens(yy * CORES + core, h)
            block = hb[h, pl.ds(T + yy * CORES, CORES), :count]
            block = block.reshape(CORES * count, feats)
            for k in range(heads_here):
                qfull[k, :, :count] = project(block, k).reshape(CORES, count, span)
                qsib[yy, h, k, :count] = qfull[k, 1 - c, :count].astype(BF16)
                query_to_sibling(yy, h, k).start()
                waits.append(query_to_sibling(yy, h, k).wait_send)
            for k in range(heads_here):
                query_to_sibling(yy, h, k).wait_recv()
                total = qfull[k, c, :count] + qsr[yy, h, k, :count].astype(F32)
                qsend[yy, h, k, :count] = total.astype(BF16)
                query_to_chip(yy, h, k, y).start()
                waits.append(query_to_chip(yy, h, k, y).wait_send)

    queries(0)

    for j in range(1, D):
        n = lax.rem(d + j, D)
        remote(pb.at[n], pb.at[D + n], p_s.at[n], p_r.at[n], {"dp": n}).wait_recv()

    def pairs_to(f):
        return remote(
            pb.at[jnp.where(f == d, f, D + f)], kvr.at[t], kv_s.at[f], kv_r.at[t], {"tensor": f}
        )

    for f in range(1, T - 1):
        pl.when(t != f)(lambda: pairs_to(f).start())
    load_cot.wait()
    load_bias.wait()
    scale = jnp.tanh(jnp.full((1, HEAD_SIZE), gate[0], F32))

    def heads_on_rows(block):
        return jnp.concatenate(
            [block[:, g * HEAD_SIZE : (g + 1) * HEAD_SIZE] for g in range(QUERY_GROUP)], axis=0
        )

    for h in range(HALVES):
        for k in range(heads_here):
            first, count = parts[h]
            rows_here = cot[first : first + count, k * span : (k + 1) * span]
            above[h, k, : QUERY_GROUP * count] = (scale * heads_on_rows(rows_here).astype(F32)).astype(BF16)

    for p in half(1):
        hidden_step(T - 1, p)
    for f in (0, T - 1):
        pl.when(t != f)(lambda: pairs_to(f).start())
    queries(1)
    total = pb[jnp.where(t == d, t, D + t)].astype(F32)
    for j in range(1, T):
        f = lax.rem(t + j, T)
        remote(kvr.at[f], kvr.at[f], kv_s.at[f], kv_r.at[f], {"tensor": f}).wait_recv()
        total = total + kvr[f].astype(F32)
    kvs[...] = total.astype(BF16)
    for h in range(HALVES):
        for k in range(heads_here):
            value = kvs[:, k * pair + HEAD_SIZE : (k + 1) * pair]
            stacked_rows = QUERY_GROUP * parts[h][1]
            wgrad[h, k, :stacked_rows] = lax.dot_general(
                above[h, k, :stacked_rows], value, NT, preferred_element_type=F32
            )

    scaling = HEAD_SIZE ** (-0.5)

    def grad_piece(f, k):
        return gb.at[f, :, pl.ds(k * pair, pair)]

    def grad_along(f, k, slot, to):
        return remote(
            grad_piece(slot, k), grad_piece(slot, k), g_s.at[f, k], g_r.at[slot, k], {"tensor": to}
        )

    def grad_across(f, k):
        return remote(
            grad_piece(f, k), grad_piece(T + d, k), gx_s.at[f, k], gx_r.at[d, k], {"dp": f}
        )

    def attend(h, k):
        value = kvs[:, k * pair + HEAD_SIZE : (k + 1) * pair]
        first_row, count = parts[h]
        attended = scale * jnp.dot(
            lows[k, : QUERY_GROUP * count], value, preferred_element_type=F32
        )
        for g in range(QUERY_GROUP):
            first = k * span + g * HEAD_SIZE
            out[first_row : first_row + count, first : first + HEAD_SIZE] = attended[
                g * count : (g + 1) * count
            ].astype(BF16)

    def attention(h, k):
        first_row, count = parts[h]
        stacked_rows = QUERY_GROUP * count
        key = kvs[:, k * pair : k * pair + HEAD_SIZE]
        grad_weights = wgrad[h, k, :stacked_rows]
        bias_rows = jnp.concatenate([bias[first_row : first_row + count, :]] * QUERY_GROUP, axis=0)
        query_to_sibling(y, h, k).wait_recv()
        query = qacc[h, k, :count] + qsr[y, h, k, :count].astype(F32)
        for j in range(1, Y):
            yy = lax.rem(y + j, Y)
            query_to_chip(yy, h, k, yy).wait_recv()
            query = query + qr[yy, h, k, :count].astype(F32)
        stacked = heads_on_rows(query.astype(BF16))
        scores = lax.dot_general(stacked, key, NT, preferred_element_type=F32) * scaling
        scores = scores + bias_rows
        exponent = jnp.exp(scores - jnp.max(scores, axis=-1, keepdims=True))
        weights = exponent * (1.0 / jnp.sum(exponent, axis=-1, keepdims=True))
        low = weights.astype(BF16)
        lows[k, :stacked_rows] = low
        value_grad = lax.dot_general(low, above[h, k, :stacked_rows], TN, preferred_element_type=F32)
        mean = jnp.sum(weights * grad_weights, axis=-1, keepdims=True)
        grad_low = (weights * (grad_weights - mean)).astype(BF16)
        key_grad = lax.dot_general(grad_low, stacked, TN, preferred_element_type=F32)
        return key_grad, value_grad

    grad_waits = []
    for h in range(HALVES):
        last = h == HALVES - 1
        for k in range(heads_here):
            key_grad, value_grad = attention(h, k)
            if h:
                key_grad = key_grad + gacc[k, 0]
                value_grad = value_grad + gacc[k, 1]
            if not last:
                gacc[k, 0] = key_grad
                gacc[k, 1] = value_grad
                attend(h, k)
                continue
            gb[t, :, k * pair : k * pair + HEAD_SIZE] = (key_grad * scaling).astype(BF16)
            gb[t, :, k * pair + HEAD_SIZE : (k + 1) * pair] = value_grad.astype(BF16)
            for j in range(1, T):
                f = lax.rem(t + j, T)
                grad_along(f, k, t, f).start()
                grad_waits.append(grad_along(f, k, t, f).wait_send)
            pl.when(t != d)(lambda: grad_across(t, k).start())
    for k in range(heads_here):
        attend(HALVES - 1, k)

    for wait in waits:
        wait()
    for h in range(PIECES):
        for k in range(T - 1):
            pl.when((t - k >= 0) & (t + 1 < T))(lambda: right(t - k, h).wait_send())
            pl.when((t + k < T) & (t >= 1))(lambda: left(t + k, h).wait_send())
        for f in range(T):
            pl.when(f != d)(lambda: across(f, h).wait_send())
    for f in range(T):
        pl.when(t != f)(lambda: pairs_to(f).wait_send())
    waits = list(grad_waits)

    def grad_arrive(f, k):
        grad_along(f, k, f, f).wait_recv()
        pl.when(f != d)(lambda: grad_across(f, k).start())

    for k in range(heads_here):
        for i in range(1, T):
            pl.when(t - i >= 0)(functools.partial(grad_arrive, t - i, k))
            pl.when(t + i < T)(functools.partial(grad_arrive, t + i, k))

    def wait_grads(n):
        for k in range(heads_here):
            remote(
                grad_piece(0, k), grad_piece(T + n, k), gx_s.at[0, k], gx_r.at[n, k], {"dp": n}
            ).wait_recv()

    def back(block, h):
        weights_part = wkv[h * part_feats : (h + 1) * part_feats, :]
        return lax.dot_general(block, weights_part, NT, preferred_element_type=F32)

    def image_to_sibling(yy, h):
        return remote(
            fsib.at[yy, h], fsr.at[yy, h], fc_s.at[yy, h], fc_r.at[yy, h], {"dp": sibling}
        )

    def image_to_owner(yy, ss, h, slot_y, slot_s):
        return remote(
            fsend.at[yy, ss, h], fr.at[slot_y, slot_s, h],
            f_s.at[yy, ss, h], f_r.at[slot_y, slot_s, h],
            {"section": ss, "dp": yy * CORES + c},
        )

    order = list(range(1, Y)) + [0]
    sections = list(range(1, S)) + [0]
    for j in order:
        yy = lax.rem(y + j, Y)
        if j:
            for core in range(CORES):
                wait_grads(yy * CORES + core)
            block = gb[pl.ds(T + yy * CORES, CORES)].reshape(CORES * image_count, 2 * kc)
            given, kept = 1 - c, c
        else:
            wait_grads(sibling)
            block = jnp.concatenate([gb[T + sibling], gb[d]], axis=0)
            given, kept = 0, 1
        for h in range(GRAD_PARTS):
            ffull[h] = back(block, h).reshape(CORES, image_count, part_feats)
            fsib[yy, h] = ffull[h, given].astype(BF16)
            image_to_sibling(yy, h).start()
            waits.append(image_to_sibling(yy, h).wait_send)
        for h in range(GRAD_PARTS):
            image_to_sibling(yy, h).wait_recv()
            fsum[...] = ffull[h, kept] + fsr[yy, h].astype(F32)
            for i in sections:
                ss = lax.rem(s + i, S)
                mine = fsum[pl.ds(pl.multiple_of(ss * rows, rows), rows), :]
                if i == 0 and j == 0:
                    grad[:, h * part_feats : (h + 1) * part_feats] = mine
                    continue
                fsend[yy, ss, h] = mine.astype(BF16)
                image_to_owner(yy, ss, h, y, s).start()
                waits.append(image_to_owner(yy, ss, h, y, s).wait_send)
    for h in range(GRAD_PARTS):
        columns = slice(h * part_feats, (h + 1) * part_feats)
        result = grad[:, columns]
        for j in order:
            yy = lax.rem(y + j, Y)
            for i in sections:
                if i == 0 and j == 0:
                    continue
                ss = lax.rem(s + i, S)
                image_to_owner(yy, ss, h, yy, ss).wait_recv()
                result = result + fr[yy, ss, h].astype(F32)
        grad[:, columns] = result

    for wait in waits:
        wait()
    for k in range(heads_here):
        for f in range(T):
            pl.when(f != d)(lambda: grad_across(f, k).wait_send())


def finish(out, grad, out_result, grad_result, out_held, grad_held, sems):
    arrays = [(out, out_held, out_result), (grad, grad_held, grad_result)]
    inward, outward = [], []
    for i, (source, held, result) in enumerate(arrays):
        inward.append(pltpu.make_async_copy(source, held, sems.at[i, 0]))
        outward.append(pltpu.make_async_copy(held, result, sems.at[i, 1]))
    for copy in inward:
        copy.start()
    for first, second in zip(inward, outward):
        first.wait()
        second.start()
    for copy in outward:
        copy.wait()


def local(sizes, hidden, w_query, key_w, value_w, image, bias, gate, cotangent):
    S, D, T = sizes
    Y = D // CORES
    tokens, feats = hidden.shape[1:]
    width = w_query.shape[2]
    kc = key_w.shape[2]
    rows = image.shape[1]
    images = S * rows
    heads = kc // HEAD_SIZE
    span = QUERY_GROUP * HEAD_SIZE
    part_rows = max(count for _, count in row_parts(tokens))
    part_feats = feats // GRAD_PARTS
    sem = lambda *n: pltpu.SemaphoreType.DMA(n)
    hbm = pl.BlockSpec(memory_space=pl.ANY)
    vmem = pl.BlockSpec(memory_space=pltpu.VMEM)
    smem = pl.BlockSpec(memory_space=pltpu.SMEM)
    out, grad = pl.pallas_call(
        functools.partial(kernel, sizes),
        out_shape=(
            jax.ShapeDtypeStruct((tokens, width), BF16),
            jax.ShapeDtypeStruct((rows, feats), F32),
        ),
        in_specs=[hbm] * 6 + [smem, hbm],
        out_specs=(vmem, vmem),
        scratch_shapes=[
            pltpu.VMEM((tokens, images), F32),
            pltpu.VMEM((feats, width), BF16),
            pltpu.VMEM((feats, 2 * kc), BF16),
            pltpu.VMEM((D * images, feats), BF16),
            pltpu.VMEM((tokens, width), BF16),
            pltpu.VMEM((HALVES, T + D, part_rows, feats), BF16),
            pltpu.VMEM((2 * D, images, 2 * kc), BF16),
            pltpu.VMEM((T, images, 2 * kc), BF16),
            pltpu.VMEM((images, 2 * kc), BF16),
            pltpu.VMEM((Y, HALVES, heads, part_rows, span), BF16),
            pltpu.VMEM((Y, HALVES, heads, part_rows, span), BF16),
            pltpu.VMEM((Y, HALVES, heads, part_rows, span), BF16),
            pltpu.VMEM((Y, HALVES, heads, part_rows, span), BF16),
            pltpu.VMEM((heads, CORES, part_rows, span), F32),
            pltpu.VMEM((HALVES, heads, part_rows, span), F32),
            pltpu.VMEM((HALVES, heads, QUERY_GROUP * part_rows, HEAD_SIZE), BF16),
            pltpu.VMEM((HALVES, heads, QUERY_GROUP * part_rows, images), F32),
            pltpu.VMEM((heads, QUERY_GROUP * part_rows, images), BF16),
            pltpu.VMEM((heads, 2, images, HEAD_SIZE), F32),
            pltpu.VMEM((T + D, images, 2 * kc), BF16),
            pltpu.VMEM((Y, GRAD_PARTS, images, part_feats), BF16),
            pltpu.VMEM((Y, GRAD_PARTS, images, part_feats), BF16),
            pltpu.VMEM((GRAD_PARTS, CORES, images, part_feats), F32),
            pltpu.VMEM((images, part_feats), F32),
            pltpu.VMEM((Y, S, GRAD_PARTS, rows, part_feats), BF16),
            pltpu.VMEM((Y, S, GRAD_PARTS, rows, part_feats), BF16),
            sem(4 + 2 * heads + HALVES),
            sem(S), sem(S), sem(Y), sem(Y), sem(Y), sem(Y),
            sem(T, PIECES), sem(T, PIECES), sem(T, PIECES), sem(T, PIECES), sem(D, PIECES),
            sem(D), sem(D), sem(T), sem(T),
            sem(Y, HALVES, heads), sem(Y, HALVES, heads),
            sem(Y, HALVES, heads), sem(Y, HALVES, heads),
            sem(T, heads), sem(T, heads), sem(T, heads), sem(D, heads),
            sem(Y, GRAD_PARTS), sem(Y, GRAD_PARTS),
            sem(Y, S, GRAD_PARTS), sem(Y, S, GRAD_PARTS),
        ],
        compiler_params=pltpu.CompilerParams(
            collective_id=0, has_side_effects=True, vmem_limit_bytes=VMEM_BYTES
        ),
    )(hidden[0], w_query[0], key_w[0], value_w[0], image[0], bias, gate, cotangent[0])
    out, grad = pl.pallas_call(
        finish,
        out_shape=(
            jax.ShapeDtypeStruct((tokens, width), BF16),
            jax.ShapeDtypeStruct((rows, feats), F32),
        ),
        in_specs=[hbm, hbm],
        out_specs=(hbm, hbm),
        scratch_shapes=[
            pltpu.VMEM((tokens, width), BF16),
            pltpu.VMEM((rows, feats), F32),
            sem(2, 2),
        ],
        compiler_params=pltpu.CompilerParams(vmem_limit_bytes=VMEM_BYTES),
    )(out, grad)
    return out[None], grad[None]


def solution(mesh):
    sizes = tuple(mesh.shape[name] for name in ("section", "dp", "tensor"))
    assert sizes[1] == sizes[2] and sizes[1] % CORES == 0
    in_specs = (
        P("section", "dp", "tensor"),
        P("section", "dp", "tensor"),
        P("section", "tensor", "dp"),
        P("section", "tensor", "dp"),
        P("dp", "section", "tensor"),
        P("dp", None),
        P("section"),
        P("section", "dp", "tensor"),
    )
    out_specs = (P("section", "dp", "tensor"), P("dp", "section", "tensor"))
    return jax.shard_map(
        functools.partial(local, sizes),
        mesh=mesh, in_specs=in_specs, out_specs=out_specs, check_vma=False,
    )
```

```python
import functools

import jax
import jax.numpy as jnp
from jax import lax
from jax.experimental import pallas as pl
from jax.experimental.pallas import tpu as pltpu
from jax.sharding import PartitionSpec as P

HEAD_SIZE = 128
QUERY_GROUP = 4
VMEM_BYTES = 64 * 1024 * 1024 - 64 * 1024
HALVES = 2
COLUMN_PARTS = 2
PIECES = HALVES * COLUMN_PARTS
GRAD_PARTS = 2
CORES = 2
BF16 = jnp.bfloat16
F32 = jnp.float32
NT = (((1,), (1,)), ((), ()))
TN = (((0,), (0,)), ((), ()))


def row_parts(tokens):
    first = tokens * 3 // 5 // 16 * 16
    return (0, first), (first, tokens - first)


def remote(src, dst, send_sem, recv_sem, device):
    return pltpu.make_async_remote_copy(
        src_ref=src,
        dst_ref=dst,
        send_sem=send_sem,
        recv_sem=recv_sem,
        device_id=device,
        device_id_type=pl.DeviceIdType.MESH,
    )


def kernel(
    sizes, hidden, w_query, key_w, value_w, image, bias_in, gate, cotangent, out, grad,
    bias, wq, wkv, img, cot, hb, pb, kvr, kvs, qsib, qsr, qsend, qr, qfull, qacc, above, wgrad, lows, gacc, gb, fsib, fsr, ffull, fsum, fsend, fr,
    load, ix_s, ix_r, iy_s, iy_r, ic_s, ic_r, hr_s, hl_s, h_r, hx_s, hx_r, p_s, p_r, kv_s, kv_r,
    qc_s, qc_r, qy_s, qy_r, g_s, g_r, gx_s, gx_r, fc_s, fc_r, f_s, f_r,
):
    S, D, T = sizes
    Y = D // CORES
    s, d, t = lax.axis_index("section"), lax.axis_index("dp"), lax.axis_index("tensor")
    y, c = d // CORES, d % CORES
    sibling = y * CORES + 1 - c
    rows = image.shape[0]
    image_count = S * rows
    kc = key_w.shape[1]
    width = wq.shape[1]
    feats = wq.shape[0]
    heads_here = kc // HEAD_SIZE
    pair = 2 * HEAD_SIZE
    span = QUERY_GROUP * HEAD_SIZE
    tokens = bias.shape[0]
    parts = row_parts(tokens)
    part_columns = feats // COLUMN_PARTS
    part_feats = feats // GRAD_PARTS
    waits = []

    def load_copy(i, src, dst):
        copy = pltpu.make_async_copy(src, dst, load.at[i])
        copy.start()
        return copy

    own_rows = pl.ds(pl.multiple_of(d * image_count + s * rows, rows), rows)
    load_image = load_copy(0, image, img.at[own_rows])
    load_hidden = [
        load_copy(
            4 + 2 * heads_here + h, hidden.at[pl.ds(*parts[h])], hb.at[h, t, pl.ds(0, parts[h][1])]
        )
        for h in range(HALVES)
    ]
    load_bias = load_copy(1, bias_in, bias)
    load_query = load_copy(2, w_query, wq)
    load_cot = load_copy(3, cotangent, cot)
    load_pairs = []
    for k in range(heads_here):
        head = pl.ds(k * HEAD_SIZE, HEAD_SIZE)
        load_pairs += [
            load_copy(4 + 2 * k, key_w.at[:, head], wkv.at[:, pl.ds(k * pair, HEAD_SIZE)]),
            load_copy(
                5 + 2 * k, value_w.at[:, head], wkv.at[:, pl.ds(k * pair + HEAD_SIZE, HEAD_SIZE)]
            ),
        ]

    others = [{"dp": lax.rem(d + j, D)} for j in range(1, D)]
    others += [{"tensor": lax.rem(t + j, T)} for j in range(1, T)]
    for i in range(1, S):
        for j in range(Y):
            others.append(
                {"section": lax.rem(s + i, S), "dp": lax.rem(y + j, Y) * CORES + c}
            )
    barrier = pltpu.get_barrier_semaphore()
    for device in others:
        pl.semaphore_signal(
            barrier, inc=1, device_id=device, device_id_type=pl.DeviceIdType.MESH
        )
    pl.semaphore_wait(barrier, len(others))

    load_image.wait()
    for i in range(1, S):
        to = lax.rem(s + i, S)
        copy = remote(
            img.at[own_rows], img.at[own_rows], ix_s.at[to], ix_r.at[s], {"section": to}
        )
        copy.start()
        waits.append(copy.wait_send)

    for load_half in load_hidden:
        load_half.wait()

    def piece(f, p):
        columns = pl.ds(p % COLUMN_PARTS * part_columns, part_columns)
        h = p // COLUMN_PARTS
        return hb.at[h, f, pl.ds(0, parts[h][1]), columns]

    def right(f, h):
        return remote(piece(f, h), piece(f, h), hr_s.at[f, h], h_r.at[f, h], {"tensor": t + 1})

    def left(f, h):
        return remote(piece(f, h), piece(f, h), hl_s.at[f, h], h_r.at[f, h], {"tensor": t - 1})

    def across(f, h):
        return remote(piece(f, h), piece(T + d, h), hx_s.at[f, h], hx_r.at[d, h], {"dp": f})

    def hidden_arrive(k, h):
        pl.when(t - k >= 0)(lambda: right(t - k, h).wait_recv())
        pl.when(t + k < T)(lambda: left(t + k, h).wait_recv())

    def hidden_pass(k, h):
        if k < T - 1:
            pl.when((t - k >= 0) & (t + 1 < T))(lambda: right(t - k, h).start())
            pl.when((t + k < T) & (t >= 1))(lambda: left(t + k, h).start())
        if k:
            pl.when((t - k >= 0) & (t - k != d))(lambda: across(t - k, h).start())
            pl.when((t + k < T) & (t + k != d))(lambda: across(t + k, h).start())

    def hidden_step(k, h):
        hidden_arrive(k, h)
        hidden_pass(k, h)

    def half(h):
        return range(h * COLUMN_PARTS, (h + 1) * COLUMN_PARTS)

    def own_across(h):
        for p in half(h):
            pl.when(t != d)(lambda: across(t, p).start())

    for p in half(0):
        hidden_pass(0, p)

    def image_block(n):
        return img.at[pl.ds(pl.multiple_of(n * image_count, image_count), image_count)]

    for i in range(1, S):
        src = lax.rem(s + i, S)
        block = img.at[pl.ds(pl.multiple_of(d * image_count + src * rows, rows), rows)]
        remote(block, block, ix_s.at[src], ix_r.at[src], {"section": src}).wait_recv()
    for j in range(1, Y):
        to = lax.rem(y + j, Y)
        copy = remote(
            image_block(d), image_block(d), iy_s.at[to], iy_r.at[y], {"dp": to * CORES + c}
        )
        copy.start()
        waits.append(copy.wait_send)

    def to_sibling(n, slot):
        copy = remote(image_block(n), image_block(n), ic_s.at[slot], ic_r.at[slot], {"dp": sibling})
        copy.start()
        waits.append(copy.wait_send)

    to_sibling(d, y)
    own_across(0)
    for k in range(1, T - 1):
        for p in half(0):
            hidden_step(k, p)
    for p in half(1):
        hidden_pass(0, p)
    for p in half(1):
        hidden_step(1, p)
    for p in half(0):
        hidden_step(T - 1, p)
    own_across(1)
    for k in range(2, T - 1):
        for p in half(1):
            hidden_step(k, p)
    for j in range(1, Y):
        src = lax.rem(y + j, Y)
        n = src * CORES + c
        remote(
            image_block(n), image_block(n), iy_s.at[src], iy_r.at[src], {"dp": n}
        ).wait_recv()
        to_sibling(n, src)

    for j in range(Y):
        n = j * CORES + 1 - c
        remote(
            image_block(n), image_block(n), ic_s.at[j], ic_r.at[j], {"dp": sibling}
        ).wait_recv()
    for load_pair in load_pairs:
        load_pair.wait()
    ptile = min(256, 2 * kc)

    @pl.loop(0, 2 * kc // ptile)
    def _(i):
        columns = pl.ds(pl.multiple_of(i * ptile, ptile), ptile)
        part = jnp.dot(img[...], wkv[:, columns], preferred_element_type=F32).astype(BF16)
        for n in range(D):
            pb[n, :, columns] = part[n * image_count : (n + 1) * image_count]

    for j in range(1, D):
        n = lax.rem(d + j, D)
        copy = remote(pb.at[n], pb.at[D + d], p_s.at[n], p_r.at[d], {"dp": n})
        copy.start()
        waits.append(copy.wait_send)


    load_query.wait()

    def wait_tokens(n, h):
        for p in half(h):
            remote(
                piece(0, p), piece(T + n, p), hx_s.at[0, p], hx_r.at[n, p], {"dp": n}
            ).wait_recv()

    def project(block, k):
        columns = slice(k * span, (k + 1) * span)
        return jnp.dot(block, wq[:, columns], preferred_element_type=F32)

    def query_to_sibling(yy, h, k):
        held = pl.ds(0, parts[h][1])
        return remote(
            qsib.at[yy, h, k, held], qsr.at[yy, h, k, held], qc_s.at[yy, h, k], qc_r.at[yy, h, k],
            {"dp": sibling},
        )

    def query_to_chip(yy, h, k, slot):
        held = pl.ds(0, parts[h][1])
        return remote(
            qsend.at[yy, h, k, held], qr.at[slot, h, k, held], qy_s.at[yy, h, k], qy_r.at[slot, h, k],
            {"dp": yy * CORES + c},
        )

    def queries(h):
        count = parts[h][1]
        wait_tokens(sibling, h)
        block = jnp.concatenate([hb[h, T + sibling, :count], hb[h, d, :count]], axis=0)
        for k in range(heads_here):
            part = project(block, k)
            qsib[y, h, k, :count] = part[:count].astype(BF16)
            query_to_sibling(y, h, k).start()
            waits.append(query_to_sibling(y, h, k).wait_send)
            qacc[h, k, :count] = part[count:]
        for j in range(1, Y):
            yy = lax.rem(y + j, Y)
            for core in range(CORES):
                wait_tokens(yy * CORES + core, h)
            block = hb[h, pl.ds(T + yy * CORES, CORES), :count]
            block = block.reshape(CORES * count, feats)
            for k in range(heads_here):
                qfull[k, :, :count] = project(block, k).reshape(CORES, count, span)
                qsib[yy, h, k, :count] = qfull[k, 1 - c, :count].astype(BF16)
                query_to_sibling(yy, h, k).start()
                waits.append(query_to_sibling(yy, h, k).wait_send)
            for k in range(heads_here):
                query_to_sibling(yy, h, k).wait_recv()
                total = qfull[k, c, :count] + qsr[yy, h, k, :count].astype(F32)
                qsend[yy, h, k, :count] = total.astype(BF16)
                query_to_chip(yy, h, k, y).start()
                waits.append(query_to_chip(yy, h, k, y).wait_send)

    queries(0)

    for j in range(1, D):
        n = lax.rem(d + j, D)
        remote(pb.at[n], pb.at[D + n], p_s.at[n], p_r.at[n], {"dp": n}).wait_recv()

    def pairs_to(f):
        return remote(
            pb.at[jnp.where(f == d, f, D + f)], kvr.at[t], kv_s.at[f], kv_r.at[t], {"tensor": f}
        )

    for f in range(1, T - 1):
        pl.when(t != f)(lambda: pairs_to(f).start())
    for f in (0, T - 1):
        pl.when(t != f)(lambda: pairs_to(f).start())
    load_cot.wait()
    load_bias.wait()
    scale = jnp.tanh(jnp.full((1, HEAD_SIZE), gate[0], F32))

    def heads_on_rows(block):
        return jnp.concatenate(
            [block[:, g * HEAD_SIZE : (g + 1) * HEAD_SIZE] for g in range(QUERY_GROUP)], axis=0
        )

    for h in range(HALVES):
        for k in range(heads_here):
            first, count = parts[h]
            rows_here = cot[first : first + count, k * span : (k + 1) * span]
            above[h, k, : QUERY_GROUP * count] = (scale * heads_on_rows(rows_here).astype(F32)).astype(BF16)

    for p in half(1):
        hidden_step(T - 1, p)
    queries(1)
    total = pb[jnp.where(t == d, t, D + t)].astype(F32)
    for j in range(1, T):
        f = lax.rem(t + j, T)
        remote(kvr.at[f], kvr.at[f], kv_s.at[f], kv_r.at[f], {"tensor": f}).wait_recv()
        total = total + kvr[f].astype(F32)
    kvs[...] = total.astype(BF16)
    for h in range(HALVES):
        for k in range(heads_here):
            value = kvs[:, k * pair + HEAD_SIZE : (k + 1) * pair]
            stacked_rows = QUERY_GROUP * parts[h][1]
            wgrad[h, k, :stacked_rows] = lax.dot_general(
                above[h, k, :stacked_rows], value, NT, preferred_element_type=F32
            )

    scaling = HEAD_SIZE ** (-0.5)

    def grad_piece(f, k):
        return gb.at[f, :, pl.ds(k * pair, pair)]

    def grad_along(f, k, slot, to):
        return remote(
            grad_piece(slot, k), grad_piece(slot, k), g_s.at[f, k], g_r.at[slot, k], {"tensor": to}
        )

    def grad_across(f, k):
        return remote(
            grad_piece(f, k), grad_piece(T + d, k), gx_s.at[f, k], gx_r.at[d, k], {"dp": f}
        )

    def attend(h, k):
        value = kvs[:, k * pair + HEAD_SIZE : (k + 1) * pair]
        first_row, count = parts[h]
        attended = scale * jnp.dot(
            lows[k, : QUERY_GROUP * count], value, preferred_element_type=F32
        )
        for g in range(QUERY_GROUP):
            first = k * span + g * HEAD_SIZE
            out[first_row : first_row + count, first : first + HEAD_SIZE] = attended[
                g * count : (g + 1) * count
            ].astype(BF16)

    def attention(h, k):
        first_row, count = parts[h]
        stacked_rows = QUERY_GROUP * count
        key = kvs[:, k * pair : k * pair + HEAD_SIZE]
        grad_weights = wgrad[h, k, :stacked_rows]
        bias_rows = jnp.concatenate([bias[first_row : first_row + count, :]] * QUERY_GROUP, axis=0)
        query_to_sibling(y, h, k).wait_recv()
        query = qacc[h, k, :count] + qsr[y, h, k, :count].astype(F32)
        for j in range(1, Y):
            yy = lax.rem(y + j, Y)
            query_to_chip(yy, h, k, yy).wait_recv()
            query = query + qr[yy, h, k, :count].astype(F32)
        stacked = heads_on_rows(query.astype(BF16))
        scores = lax.dot_general(stacked, key, NT, preferred_element_type=F32) * scaling
        scores = scores + bias_rows
        exponent = jnp.exp(scores - jnp.max(scores, axis=-1, keepdims=True))
        weights = exponent * (1.0 / jnp.sum(exponent, axis=-1, keepdims=True))
        low = weights.astype(BF16)
        lows[k, :stacked_rows] = low
        value_grad = lax.dot_general(low, above[h, k, :stacked_rows], TN, preferred_element_type=F32)
        mean = jnp.sum(weights * grad_weights, axis=-1, keepdims=True)
        grad_low = (weights * (grad_weights - mean)).astype(BF16)
        key_grad = lax.dot_general(grad_low, stacked, TN, preferred_element_type=F32)
        return key_grad, value_grad

    grad_waits = []
    for h in range(HALVES):
        last = h == HALVES - 1
        for k in range(heads_here):
            key_grad, value_grad = attention(h, k)
            if h:
                key_grad = key_grad + gacc[k, 0]
                value_grad = value_grad + gacc[k, 1]
            if not last:
                gacc[k, 0] = key_grad
                gacc[k, 1] = value_grad
                attend(h, k)
                continue
            gb[t, :, k * pair : k * pair + HEAD_SIZE] = (key_grad * scaling).astype(BF16)
            gb[t, :, k * pair + HEAD_SIZE : (k + 1) * pair] = value_grad.astype(BF16)
            for j in range(1, T):
                f = lax.rem(t + j, T)
                grad_along(f, k, t, f).start()
                grad_waits.append(grad_along(f, k, t, f).wait_send)
            pl.when(t != d)(lambda: grad_across(t, k).start())
    for k in range(heads_here):
        attend(HALVES - 1, k)

    for wait in waits:
        wait()
    for h in range(PIECES):
        for k in range(T - 1):
            pl.when((t - k >= 0) & (t + 1 < T))(lambda: right(t - k, h).wait_send())
            pl.when((t + k < T) & (t >= 1))(lambda: left(t + k, h).wait_send())
        for f in range(T):
            pl.when(f != d)(lambda: across(f, h).wait_send())
    for f in range(T):
        pl.when(t != f)(lambda: pairs_to(f).wait_send())
    waits = list(grad_waits)

    def grad_arrive(f, k):
        grad_along(f, k, f, f).wait_recv()
        pl.when(f != d)(lambda: grad_across(f, k).start())

    for k in range(heads_here):
        for i in range(1, T):
            pl.when(t - i >= 0)(functools.partial(grad_arrive, t - i, k))
            pl.when(t + i < T)(functools.partial(grad_arrive, t + i, k))

    def wait_grads(n):
        for k in range(heads_here):
            remote(
                grad_piece(0, k), grad_piece(T + n, k), gx_s.at[0, k], gx_r.at[n, k], {"dp": n}
            ).wait_recv()

    def back(block, h):
        weights_part = wkv[h * part_feats : (h + 1) * part_feats, :]
        return lax.dot_general(block, weights_part, NT, preferred_element_type=F32)

    def image_to_sibling(yy, h):
        return remote(
            fsib.at[yy, h], fsr.at[yy, h], fc_s.at[yy, h], fc_r.at[yy, h], {"dp": sibling}
        )

    def image_to_owner(yy, ss, h, slot_y, slot_s):
        return remote(
            fsend.at[yy, ss, h], fr.at[slot_y, slot_s, h],
            f_s.at[yy, ss, h], f_r.at[slot_y, slot_s, h],
            {"section": ss, "dp": yy * CORES + c},
        )

    order = list(range(1, Y)) + [0]
    sections = list(range(1, S)) + [0]
    for j in order:
        yy = lax.rem(y + j, Y)
        if j:
            for core in range(CORES):
                wait_grads(yy * CORES + core)
            block = gb[pl.ds(T + yy * CORES, CORES)].reshape(CORES * image_count, 2 * kc)
            given, kept = 1 - c, c
        else:
            wait_grads(sibling)
            block = jnp.concatenate([gb[T + sibling], gb[d]], axis=0)
            given, kept = 0, 1
        for h in range(GRAD_PARTS):
            ffull[h] = back(block, h).reshape(CORES, image_count, part_feats)
            fsib[yy, h] = ffull[h, given].astype(BF16)
            image_to_sibling(yy, h).start()
            waits.append(image_to_sibling(yy, h).wait_send)
        for h in range(GRAD_PARTS):
            image_to_sibling(yy, h).wait_recv()
            fsum[...] = ffull[h, kept] + fsr[yy, h].astype(F32)
            for i in sections:
                ss = lax.rem(s + i, S)
                mine = fsum[pl.ds(pl.multiple_of(ss * rows, rows), rows), :]
                if i == 0 and j == 0:
                    grad[:, h * part_feats : (h + 1) * part_feats] = mine
                    continue
                fsend[yy, ss, h] = mine.astype(BF16)
                image_to_owner(yy, ss, h, y, s).start()
                waits.append(image_to_owner(yy, ss, h, y, s).wait_send)
    for h in range(GRAD_PARTS):
        columns = slice(h * part_feats, (h + 1) * part_feats)
        result = grad[:, columns]
        for j in order:
            yy = lax.rem(y + j, Y)
            for i in sections:
                if i == 0 and j == 0:
                    continue
                ss = lax.rem(s + i, S)
                image_to_owner(yy, ss, h, yy, ss).wait_recv()
                result = result + fr[yy, ss, h].astype(F32)
        grad[:, columns] = result

    for wait in waits:
        wait()
    for k in range(heads_here):
        for f in range(T):
            pl.when(f != d)(lambda: grad_across(f, k).wait_send())


def finish(out, grad, out_result, grad_result, out_held, grad_held, sems):
    arrays = [(out, out_held, out_result), (grad, grad_held, grad_result)]
    inward, outward = [], []
    for i, (source, held, result) in enumerate(arrays):
        inward.append(pltpu.make_async_copy(source, held, sems.at[i, 0]))
        outward.append(pltpu.make_async_copy(held, result, sems.at[i, 1]))
    for copy in inward:
        copy.start()
    for first, second in zip(inward, outward):
        first.wait()
        second.start()
    for copy in outward:
        copy.wait()


def local(sizes, hidden, w_query, key_w, value_w, image, bias, gate, cotangent):
    S, D, T = sizes
    Y = D // CORES
    tokens, feats = hidden.shape[1:]
    width = w_query.shape[2]
    kc = key_w.shape[2]
    rows = image.shape[1]
    images = S * rows
    heads = kc // HEAD_SIZE
    span = QUERY_GROUP * HEAD_SIZE
    part_rows = max(count for _, count in row_parts(tokens))
    part_feats = feats // GRAD_PARTS
    sem = lambda *n: pltpu.SemaphoreType.DMA(n)
    hbm = pl.BlockSpec(memory_space=pl.ANY)
    vmem = pl.BlockSpec(memory_space=pltpu.VMEM)
    smem = pl.BlockSpec(memory_space=pltpu.SMEM)
    out, grad = pl.pallas_call(
        functools.partial(kernel, sizes),
        out_shape=(
            jax.ShapeDtypeStruct((tokens, width), BF16),
            jax.ShapeDtypeStruct((rows, feats), F32),
        ),
        in_specs=[hbm] * 6 + [smem, hbm],
        out_specs=(vmem, vmem),
        scratch_shapes=[
            pltpu.VMEM((tokens, images), F32),
            pltpu.VMEM((feats, width), BF16),
            pltpu.VMEM((feats, 2 * kc), BF16),
            pltpu.VMEM((D * images, feats), BF16),
            pltpu.VMEM((tokens, width), BF16),
            pltpu.VMEM((HALVES, T + D, part_rows, feats), BF16),
            pltpu.VMEM((2 * D, images, 2 * kc), BF16),
            pltpu.VMEM((T, images, 2 * kc), BF16),
            pltpu.VMEM((images, 2 * kc), BF16),
            pltpu.VMEM((Y, HALVES, heads, part_rows, span), BF16),
            pltpu.VMEM((Y, HALVES, heads, part_rows, span), BF16),
            pltpu.VMEM((Y, HALVES, heads, part_rows, span), BF16),
            pltpu.VMEM((Y, HALVES, heads, part_rows, span), BF16),
            pltpu.VMEM((heads, CORES, part_rows, span), F32),
            pltpu.VMEM((HALVES, heads, part_rows, span), F32),
            pltpu.VMEM((HALVES, heads, QUERY_GROUP * part_rows, HEAD_SIZE), BF16),
            pltpu.VMEM((HALVES, heads, QUERY_GROUP * part_rows, images), F32),
            pltpu.VMEM((heads, QUERY_GROUP * part_rows, images), BF16),
            pltpu.VMEM((heads, 2, images, HEAD_SIZE), F32),
            pltpu.VMEM((T + D, images, 2 * kc), BF16),
            pltpu.VMEM((Y, GRAD_PARTS, images, part_feats), BF16),
            pltpu.VMEM((Y, GRAD_PARTS, images, part_feats), BF16),
            pltpu.VMEM((GRAD_PARTS, CORES, images, part_feats), F32),
            pltpu.VMEM((images, part_feats), F32),
            pltpu.VMEM((Y, S, GRAD_PARTS, rows, part_feats), BF16),
            pltpu.VMEM((Y, S, GRAD_PARTS, rows, part_feats), BF16),
            sem(4 + 2 * heads + HALVES),
            sem(S), sem(S), sem(Y), sem(Y), sem(Y), sem(Y),
            sem(T, PIECES), sem(T, PIECES), sem(T, PIECES), sem(T, PIECES), sem(D, PIECES),
            sem(D), sem(D), sem(T), sem(T),
            sem(Y, HALVES, heads), sem(Y, HALVES, heads),
            sem(Y, HALVES, heads), sem(Y, HALVES, heads),
            sem(T, heads), sem(T, heads), sem(T, heads), sem(D, heads),
            sem(Y, GRAD_PARTS), sem(Y, GRAD_PARTS),
            sem(Y, S, GRAD_PARTS), sem(Y, S, GRAD_PARTS),
        ],
        compiler_params=pltpu.CompilerParams(
            collective_id=0, has_side_effects=True, vmem_limit_bytes=VMEM_BYTES
        ),
    )(hidden[0], w_query[0], key_w[0], value_w[0], image[0], bias, gate, cotangent[0])
    out, grad = pl.pallas_call(
        finish,
        out_shape=(
            jax.ShapeDtypeStruct((tokens, width), BF16),
            jax.ShapeDtypeStruct((rows, feats), F32),
        ),
        in_specs=[hbm, hbm],
        out_specs=(hbm, hbm),
        scratch_shapes=[
            pltpu.VMEM((tokens, width), BF16),
            pltpu.VMEM((rows, feats), F32),
            sem(2, 2),
        ],
        compiler_params=pltpu.CompilerParams(vmem_limit_bytes=VMEM_BYTES),
    )(out, grad)
    return out[None], grad[None]


def solution(mesh):
    sizes = tuple(mesh.shape[name] for name in ("section", "dp", "tensor"))
    assert sizes[1] == sizes[2] and sizes[1] % CORES == 0
    in_specs = (
        P("section", "dp", "tensor"),
        P("section", "dp", "tensor"),
        P("section", "tensor", "dp"),
        P("section", "tensor", "dp"),
        P("dp", "section", "tensor"),
        P("dp", None),
        P("section"),
        P("section", "dp", "tensor"),
    )
    out_specs = (P("section", "dp", "tensor"), P("dp", "section", "tensor"))
    return jax.shard_map(
        functools.partial(local, sizes),
        mesh=mesh, in_specs=in_specs, out_specs=out_specs, check_vma=False,
    )
```
